128 devices in a mesh: gx: 8 (over z, core), yz: 16 (over x, y).
Axes of the slice: x: 4, y: 4, z: 4, core: 2. Of those that a mesh axis runs over, the one named last changes fastest.
Arguments:
- starting_warmth_level: float32 [64, 128, 1024], P('gx', 'yz'), may hold values from -6 to 6
- diffusive_coefficient_map: float32 [64, 128, 1024], P('gx', 'yz'), may hold values from 0.5 to 8
- specific_warmth_store: float32 [64, 128, 1024], P('gx', 'yz'), may hold values from 0.25 to 2
- energy_source_flux: float32 [64, 128, 1024], P('gx', 'yz'), may hold values from -6 to 6
- deformation_vector: float32 [3, 64, 128, 1024], P(None, 'gx', 'yz'), may hold values from -6 to 6
- substance_label_columns: int32 [64, 128], P('gx'), may hold values from 0 to 1
- substance_moduli_table: float32 [2, 2], replicated, may hold values from 0.5 to 2
- subdomain_point_tally: int32 [16], replicated, may hold values from 1 to 128, 1024 in all
Outputs:
- final_warmth_level: float32 [64, 128, 1024], P('gx', 'yz')
- residual: float32 [3, 64, 128, 2048], P(None, 'gx', None, 'yz')
The draws below stay inside these ranges and needn't reach their ends.
Inputs may be any that keep to these rules, and one draw needn't show every extreme that they name: `subdomain_point_tally`: the lengths sum to 1024, and some part has exactly 128 nodes.
All inputs are finite; a program needn't handle non-finite values.
Results may differ from the reference program's by a relative error of at most 0.00026.
Values sent between devices are 32-bit elements; how exact they have to be, the bound alone decides.
A program may use at most 128 MiB of HBM per device.

```python
import math
import jax
import jax.numpy as jnp
import numpy as np

NCHEB = 6
STEPS = 2
NMAT = 2
ZMAX = 128
PARTS_SIZE = 16
LATTICE_COUNT_I = 64
LATTICE_COUNT_J = 128
LATTICE_COUNT_K = 1024


def set_ends(entries, own_key, least, largest):
    longest = entries.shape.index(max(entries.shape))
    spots = []
    for shift in (0, 1):
        where = [jax.random.randint(jax.random.fold_in(own_key, axis), (), 0, length) for axis, length in enumerate(entries.shape)]
        where[longest] = (where[longest] + shift) % entries.shape[longest]
        spots.append(tuple(where))
    return entries.at[spots[0]].set(least).at[spots[1]].set(largest)


def shard_levels(stream_key, extent, pieces, smallest, top_value):
    loudness = 1.0
    for axis_at, shards_of in pieces:
        steps = jax.random.uniform(jax.random.fold_in(jax.random.fold_in(stream_key, 6), axis_at), (shards_of,), jnp.float32, smallest / len(pieces), top_value / len(pieces))
        loudness = loudness * jnp.repeat(jnp.exp(steps), extent[axis_at] // shards_of).reshape((-1,) + (1,) * (len(extent) - 1 - axis_at))
    return loudness


def length_profile(amount, total, reach, lean):
    weights = [(1 << 20) // math.isqrt(standing ** lean) + 1 for standing in range(2, amount + 1)]
    rest, counts = total - reach - (amount - 1), [1] * (amount - 1)
    while rest > 0:
        candidates = [i for i in range(amount - 1) if counts[i] < reach]
        mass, budget = sum([weights[i] for i in candidates]), rest
        for i in candidates:
            more = min(reach - counts[i], max(1, budget * weights[i] // mass), rest)
            counts[i] = counts[i] + more
            rest = rest - more
    return np.array([reach] + counts)


def ragged(rng, count, total, bound, lean):
    if count == 2:
        one = jax.random.randint(rng, (), max(1, total - bound), min(bound, total - 1) + 1)
        return jnp.stack([one, total - one])
    lengths = jnp.asarray(length_profile(count, total, bound, lean), jnp.int32)
    twos = (count - 1) // 2
    source_of, taker = lengths[1:1 + 2 * twos:2], lengths[2:2 + 2 * twos:2]
    room = jnp.minimum(source_of - 1, bound - taker)
    passed = jax.random.randint(jax.random.fold_in(rng, 1), (twos,), 0, 1 << 20) % (room + 1)
    lengths = lengths.at[1:1 + 2 * twos:2].set(source_of - passed).at[2:2 + 2 * twos:2].set(taker + passed)
    return lengths[jax.random.permutation(jax.random.fold_in(rng, 2), count)]


def scatter_about(key, extent, scale, bound, cuts=(), held_as=jnp.bfloat16):
    loudness = shard_levels(key, extent, cuts, -0.22, 0.18) if cuts else 1.0
    array = jax.random.normal(key, extent, jnp.float32) * scale * loudness
    return jnp.minimum(jnp.maximum(array, -bound), bound).astype(held_as)


def setup_inputs(seed: int = 0) -> dict:
    seeds = jax.random.split(jax.random.key(seed), 9)
    starting_warmth_level = scatter_about(seeds[0], (LATTICE_COUNT_I, LATTICE_COUNT_J, LATTICE_COUNT_K), 1.0, 6.0, ((0, 8), (1, 16)), jnp.float32)
    diffusive_coefficient_map = jnp.clip(jnp.exp(math.log(8.0) - 2.7725887 * jax.random.uniform(seeds[1], (LATTICE_COUNT_I, LATTICE_COUNT_J, LATTICE_COUNT_K), jnp.float32) ** shard_levels(seeds[1], (LATTICE_COUNT_I, LATTICE_COUNT_J, LATTICE_COUNT_K), ((0, 8), (1, 16)), -0.2, 0.2)), 0.5, 8.0)
    specific_warmth_store = jnp.clip(jnp.exp(math.log(2.0) - 2.0794415 * jax.random.uniform(seeds[2], (LATTICE_COUNT_I, LATTICE_COUNT_J, LATTICE_COUNT_K), jnp.float32) ** shard_levels(seeds[2], (LATTICE_COUNT_I, LATTICE_COUNT_J, LATTICE_COUNT_K), ((0, 8), (1, 16)), -0.2, 0.2)), 0.25, 2.0)
    energy_source_flux = scatter_about(seeds[3], (LATTICE_COUNT_I, LATTICE_COUNT_J, LATTICE_COUNT_K), 1.0, 6.0, ((0, 8), (1, 16)), jnp.float32)
    deformation_vector = scatter_about(seeds[4], (3, LATTICE_COUNT_I, LATTICE_COUNT_J, LATTICE_COUNT_K), 1.0, 6.0, ((1, 8), (2, 16)), jnp.float32)
    substance_label_columns = set_ends(jax.random.randint(seeds[5], (LATTICE_COUNT_I, LATTICE_COUNT_J), 0, NMAT), jax.random.fold_in(seeds[5], 1), 0, NMAT - 1).astype(jnp.int32)
    substance_moduli_table = jnp.clip(jax.random.uniform(seeds[6], (2, NMAT), jnp.float32, 0.5, 2.0), 0.5, 2.0)
    subdomain_point_tally = ragged(seeds[7], PARTS_SIZE, LATTICE_COUNT_K, ZMAX, 2).astype(jnp.int32)
    return dict(starting_warmth_level=starting_warmth_level, diffusive_coefficient_map=diffusive_coefficient_map, specific_warmth_store=specific_warmth_store, energy_source_flux=energy_source_flux, deformation_vector=deformation_vector, substance_label_columns=substance_label_columns, substance_moduli_table=substance_moduli_table, subdomain_point_tally=subdomain_point_tally)


time_step = 1.0


def harmonic(first, second):
    return 2.0 * first * second / (first + second)


def neighbours(padded_field):
    return [padded_field[2:, 1:-1, 1:-1], padded_field[:-2, 1:-1, 1:-1],
            padded_field[1:-1, 2:, 1:-1], padded_field[1:-1, :-2, 1:-1],
            padded_field[1:-1, 1:-1, 2:], padded_field[1:-1, 1:-1, :-2]]


def apply_heat(field, coefs, specific_warmth_store):
    beside_all = neighbours(jnp.pad(field, 1))
    total = jnp.zeros_like(field)
    for coef, other in zip(coefs, beside_all):
        total = total + coef * (field - other)
    return specific_warmth_store * field + time_step * total


def chebyshev(rhs, start, coefs, specific_warmth_store, low, high):
    theta = (high + low) / 2.0
    delta = (high - low) / 2.0
    sigma = theta / delta
    rho = 1.0 / sigma
    solution = start
    resid = rhs - apply_heat(solution, coefs, specific_warmth_store)
    direction = resid / theta
    for turn in range(NCHEB):
        solution = solution + direction
        resid = resid - apply_heat(direction, coefs, specific_warmth_store)
        rho_new = 1.0 / (2.0 * sigma - rho)
        direction = rho_new * rho * direction + (2.0 * rho_new / delta) * resid
        rho = rho_new
    return solution


def lookup(substance_label_columns, row):
    total = jnp.zeros(substance_label_columns.shape, jnp.float32)
    for index in range(NMAT):
        total = total + jnp.where(substance_label_columns == index, row[index], 0.0)
    return total


def reference(starting_warmth_level, diffusive_coefficient_map, specific_warmth_store, energy_source_flux, deformation_vector, substance_label_columns, substance_moduli_table, subdomain_point_tally):
    kpad = jnp.pad(diffusive_coefficient_map, 1)
    coefs = [harmonic(diffusive_coefficient_map, other) for other in neighbours(kpad)]
    low = jnp.min(specific_warmth_store)
    summed = coefs[0] + coefs[1] + coefs[2] + coefs[3] + coefs[4] + coefs[5]
    high = jnp.max(specific_warmth_store + 2.0 * time_step * summed)
    final_warmth_level = starting_warmth_level
    for step in range(STEPS):
        rhs = specific_warmth_store * final_warmth_level + time_step * energy_source_flux
        final_warmth_level = chebyshev(rhs, final_warmth_level, coefs, specific_warmth_store, low, high)
    shear = lookup(substance_label_columns, substance_moduli_table[0])[:, :, None]
    beta = lookup(substance_label_columns, substance_moduli_table[1])[:, :, None]
    stress = beta * final_warmth_level
    spad = jnp.pad(stress, 1)
    snb = neighbours(spad)
    parts = []
    for comp in range(3):
        beside_all = neighbours(jnp.pad(deformation_vector[comp], 1))
        lap = 6.0 * deformation_vector[comp] - (beside_all[0] + beside_all[1] + beside_all[2] + beside_all[3] + beside_all[4] + beside_all[5])
        parts.append(shear * lap + 0.5 * (snb[2 * comp] - snb[2 * comp + 1]))
    whole = jnp.stack(parts, 0)
    starts = (jnp.cumsum(subdomain_point_tally) - subdomain_point_tally).astype(jnp.int32)
    offsets = jnp.arange(ZMAX, dtype=jnp.int32)
    where_from = (starts[:, None] + offsets[None, :]).reshape(-1).astype(jnp.int32)
    valid = (offsets[None, :] < subdomain_point_tally[:, None]).reshape(-1).astype(jnp.float32)
    padded_field = jnp.pad(whole, ((0, 0), (0, 0), (0, 0), (0, ZMAX)))
    packed = jnp.take(padded_field, where_from, axis=3) * valid
    return final_warmth_level, packed
```

```python
import functools

import jax
import jax.numpy as jnp
from jax import lax
from jax.experimental import pallas as pl
from jax.experimental.pallas import tpu as pltpu
from jax.sharding import PartitionSpec as P

NCHEB = 6
ZMAX = 128
NG, NY = 8, 16
B = 8
H = 6
N = B + 2 * H
LO, HI = H, H + B
KT = 8
LEVELS = NCHEB - 1
MESH = pl.DeviceIdType.MESH
F32 = jnp.float32


def corner_rects(width):
    if width == 6:
        return [(1, 2, 5), (3, 5, 3)]
    if width == 5:
        return [(1, 2, 4), (3, 4, 2)]
    return []


def kernel(
    x0_hbm, k_hbm, c_hbm, f_hbm, u_hbm, lab, table, tally,
    t_out, r_out,
    nat, natu, kb, cb, xb, fb, v0, v1, e, rb, fx, fy, fz, db,
    ust, uest, u, ue, tst, test, t, te, natt, ytr,
    mu, beta, ar1, ar2, arst, coefs, starts,
    lsem, lusem, hs, hr, a1s, a1r, a2s, a2r, us, ur, ues, uer, ts, tr, tes, ter, ps, pr, osem,
):
    g, y = lax.axis_index("gx"), lax.axis_index("yz")
    gp, gm = lax.rem(g + 1, NG), lax.rem(g + NG - 1, NG)
    yp, ym = lax.rem(y + 1, NY), lax.rem(y + NY - 1, NY)
    along_y = [(g, lax.rem(y + k, NY)) for k in range(1, NY)]
    along_g = [(lax.rem(g + k, NG), y) for k in range(1, NG)]
    diagonal = [(gp, yp), (gm, ym), (gp, ym), (gm, yp)]

    fields = [k_hbm, x0_hbm, c_hbm, f_hbm]
    own_in = [
        [
            pltpu.make_async_copy(
                field.at[:, :, pl.ds(kt * 128, 128)], nat.at[n, :, pl.ds(kt * 8, 8)], lsem.at[n, kt]
            )
            for kt in range(KT)
        ]
        for n, field in enumerate(fields)
    ]
    u_in = [
        pltpu.make_async_copy(
            u_hbm.at[:, :, :, pl.ds(kt * 128, 128)], natu.at[:, :, kt + 1], lusem.at[kt]
        )
        for kt in range(KT)
    ]
    for copies in own_in:
        for copy in copies:
            copy.start()
    for copy in u_in:
        copy.start()

    barrier = pltpu.get_barrier_semaphore()
    for peer in along_y + along_g + diagonal:
        pl.semaphore_signal(barrier, inc=1, device_id=peer, device_id_type=MESH)

    zero_tile = jnp.zeros((8, 128), F32)
    for a in range(3):
        def zero_u(i, _, a=a):
            u[a, i, pl.ds(0, 8)] = zero_tile
            u[a, i, pl.ds(8 + 128, 8)] = zero_tile
            return 0
        lax.fori_loop(0, B + 2, zero_u, 0)

        def zero_natu(i, _, a=a):
            natu[a, i, 0] = zero_tile
            natu[a, i, KT + 1] = zero_tile
            return 0
        lax.fori_loop(0, B, zero_natu, 0)

    def zero_t(i, _):
        t[i, pl.ds(0, 8)] = zero_tile
        t[i, pl.ds(8 + 128, 8)] = zero_tile
        return 0
    lax.fori_loop(0, B + 2, zero_t, 0)

    def zero_natt(i, _):
        natt[i, 0] = zero_tile
        natt[i, KT + 1] = zero_tile
        return 0
    lax.fori_loop(0, B, zero_natt, 0)

    def to_lines(n, dst):
        def row(i, _):
            for j in range(B):
                dst[LO + i, LO + j] = nat[n, i, pl.ds(j, 8, stride=8), :]
            return 0
        lax.fori_loop(0, B, row, 0)

    for n, dst in ((0, kb), (1, xb), (2, cb), (3, fb)):
        for copy in own_in[n]:
            copy.wait()
        to_lines(n, dst)

    pl.semaphore_wait(barrier, len(along_y) + len(along_g) + len(diagonal))

    def halo(buf, width, slot):
        own, low, high = pl.ds(LO, B), pl.ds(LO - width, width), pl.ds(HI, width)
        first, last = pl.ds(LO, width), pl.ds(HI - width, width)
        moves = [
            (buf.at[own, last], buf.at[own, low], (g, yp)),
            (buf.at[own, first], buf.at[own, high], (g, ym)),
            (buf.at[last, own], buf.at[low, own], (gp, y)),
            (buf.at[first, own], buf.at[high, own], (gm, y)),
        ]
        for a0, a1, b1 in corner_rects(width):
            rows = a1 - a0 + 1
            li, lj = LO - a1, LO - b1
            hi, hj = HI - 1 + a0, HI
            for peer, i, j, si, sj in (
                ((gp, yp), li, lj, B, B),
                ((gm, ym), hi, hj, -B, -B),
                ((gp, ym), li, hj, B, -B),
                ((gm, yp), hi, lj, -B, B),
            ):
                moves.append(
                    (
                        buf.at[pl.ds(i + si, rows), pl.ds(j + sj, b1)],
                        buf.at[pl.ds(i, rows), pl.ds(j, b1)],
                        peer,
                    )
                )
        return [
            pltpu.make_async_remote_copy(
                src_ref=src, dst_ref=dst, send_sem=hs.at[slot, m], recv_sem=hr.at[slot, m],
                device_id=peer, device_id_type=MESH,
            )
            for m, (src, dst, peer) in enumerate(moves)
        ]

    x0_moves, k_moves, c_moves = halo(xb, 1, 0), halo(kb, 6, 1), halo(cb, 5, 2)
    for copy in x0_moves + k_moves + c_moves:
        copy.start()

    total = jnp.int32(0)
    for p in range(NY):
        starts[p] = total
        total = total + tally[p]

    eye = lax.broadcasted_iota(jnp.int32, (128, 128), 0) == lax.broadcasted_iota(jnp.int32, (128, 128), 1)

    def column_row(i, _):
        row = jnp.broadcast_to(lab[pl.ds(i, 1), :].astype(F32), (128, 128))
        column = jnp.sum(jnp.where(eye, row, 0.0), axis=1, keepdims=True)
        label = jnp.broadcast_to(column, (128, 128))
        for dst, r in ((mu, 0), (beta, 1)):
            dst[i] = jnp.where(label == 0.0, table[r, 0], 0.0) + jnp.where(label == 1.0, table[r, 1], 0.0)
        return 0
    lax.fori_loop(0, B, column_row, 0)

    lane = lax.broadcasted_iota(jnp.int32, (8, 128), 1)

    def pack(line, p, lane_of):
        start = starts[p]
        tile, off = start >> 7, start & 127
        window = jnp.where(lane >= off, line[tile + 1], line[tile + 2])
        before = start - 1 + 128
        after = start + tally[p] + 128
        prev = pltpu.roll(line[before >> 7], (lane_of - (before & 127) + 256) & 127, 1)
        nxt = pltpu.roll(line[after >> 7], (32 + lane_of - (after & 127) + 256) & 127, 1)
        return pltpu.roll(window, (128 - off) & 127, 1), prev, nxt

    for copy in u_in:
        copy.wait()

    def pack_u(p, _):
        edge = zero_tile
        for a in range(3):
            def one(i, edge, a=a):
                at = a * 8 + i
                window, prev, nxt = pack(natu.at[a, i], p, at)
                ust[p, a, i] = window
                return jnp.where(lane == at, prev, jnp.where(lane == at + 32, nxt, edge))
            edge = lax.fori_loop(0, B, one, edge)
        uest[p] = edge
        return 0
    lax.fori_loop(0, NY, pack_u, 0)

    def iota(n, axis):
        return lax.broadcasted_iota(jnp.int32, (n, 8, 128), axis)

    def up(v):
        by_lane = pltpu.roll(v, 127, 2)
        return jnp.where(iota(v.shape[0], 2) == 127, pltpu.roll(by_lane, 7, 1), by_lane)

    def down(v):
        by_lane = pltpu.roll(v, 1, 2)
        return jnp.where(iota(v.shape[0], 2) == 0, pltpu.roll(by_lane, 1, 1), by_lane)

    def harmonic(first, second):
        return 2.0 * first * second / (first + second)

    inside_low_g = jnp.where(g > 0, 1.0, 0.0)
    inside_high_g = jnp.where(g < NG - 1, 1.0, 0.0)
    inside_low_y = jnp.where(y > 0, 1.0, 0.0)
    inside_high_y = jnp.where(y < NY - 1, 1.0, 0.0)

    def faces(q):
        lo, n = LO - q, B + 2 * q
        half = n // 2
        chunks = [(lo, half), (lo + half, n - half)]

        def fx_row(i, _):
            for j0, c in chunks:
                at = pl.ds(j0, c)
                fx[i, at] = harmonic(kb[i, at], kb[i + 1, at])
            return 0
        lax.fori_loop(lo - 1, lo + n, fx_row, 0)

        fx[LO - 1, pl.ds(lo, n)] = fx[LO - 1, pl.ds(lo, n)] * inside_low_g
        fx[HI - 1, pl.ds(lo, n)] = fx[HI - 1, pl.ds(lo, n)] * inside_high_g

        def row(i, _):
            fy[i, lo - 1] = harmonic(kb[i, lo - 1], kb[i, lo])
            for j0, c in chunks:
                at = pl.ds(j0, c)
                own = kb[i, at]
                fy[i, at] = harmonic(own, kb[i, pl.ds(j0 + 1, c)])
                last = (iota(c, 1) == 7) & (iota(c, 2) == 127)
                fz[i, at] = jnp.where(last, 0.0, harmonic(own, up(own)))
            fy[i, LO - 1] = fy[i, LO - 1] * inside_low_y
            fy[i, HI - 1] = fy[i, HI - 1] * inside_high_y
            for j0, c in chunks:
                at = pl.ds(j0, c)
                z = fz[i, at]
                db[i, at] = (
                    cb[i, at] + fx[i, at] + fx[i - 1, at] + fy[i, at] + fy[i, pl.ds(j0 - 1, c)] + z + down(z)
                )
            return 0
        lax.fori_loop(lo, lo + n, row, 0)

    def applied(v, i, j0, c):
        at = pl.ds(j0, c)
        own, z = v[i, at], fz[i, at]
        return (
            db[i, at] * own
            - fx[i, at] * v[i + 1, at]
            - fx[i - 1, at] * v[i - 1, at]
            - fy[i, at] * v[i, pl.ds(j0 + 1, c)]
            - fy[i, pl.ds(j0 - 1, c)] * v[i, pl.ds(j0 - 1, c)]
            - z * up(own)
            - down(z * own)
        )

    def first_residual(x, dst):
        def row(i, _):
            at = pl.ds(LO, B)
            dst[i, at] = fb[i, at] + (cb[i, at] * x[i, at] - applied(x, i, LO, B))
            return 0
        lax.fori_loop(LO, HI, row, 0)

    for copy in x0_moves + k_moves[:4]:
        copy.wait_recv()
    faces(0)

    def bound_row(i, carry):
        most, least = carry
        at = pl.ds(LO, B)
        c = cb[i, at]
        return (
            jnp.maximum(most, jnp.max(2.0 * db[i, at] - c, axis=0)),
            jnp.maximum(least, jnp.max(-c, axis=0)),
        )
    neg = jnp.full((8, 128), -3.0e38, F32)
    most, least = lax.fori_loop(LO, HI, bound_row, (neg, neg))
    sub = lax.broadcasted_iota(jnp.int32, (8, 128), 0)

    def over_rows(v):
        return jnp.broadcast_to(jnp.max(v, axis=0, keepdims=True), (8, 128))

    arst[0] = jnp.where(sub < 4, over_rows(most), over_rows(least))
    ar1[y] = arst[0]
    ar1_moves = [
        pltpu.make_async_remote_copy(
            src_ref=arst.at[0], dst_ref=ar1.at[y], send_sem=a1s.at[k], recv_sem=a1r.at[k],
            device_id=peer, device_id_type=MESH,
        )
        for k, peer in enumerate(along_y)
    ]
    for copy in ar1_moves:
        copy.start()

    first_residual(xb, v0)
    v0_moves = halo(v0, 6, 3)
    for copy in v0_moves:
        copy.start()

    rows_of_me = pl.ds(pl.multiple_of(8 + 8 * y, 8), 8)

    def u_copies(k):
        p = lax.rem(y + k, NY)
        peer = (g, p)
        return [
            pltpu.make_async_remote_copy(
                src_ref=ust.at[p], dst_ref=u.at[:, pl.ds(1, B), rows_of_me],
                send_sem=us.at[k], recv_sem=ur.at[k], device_id=peer, device_id_type=MESH,
            ),
            pltpu.make_async_remote_copy(
                src_ref=uest.at[p], dst_ref=ue.at[rows_of_me],
                send_sem=ues.at[k], recv_sem=uer.at[k], device_id=peer, device_id_type=MESH,
            ),
        ]

    u_moves = [u_copies(k) for k in range(1, NY)]
    u_own = [
        pltpu.make_async_copy(ust.at[y], u.at[:, pl.ds(1, B), rows_of_me], us.at[0]),
        pltpu.make_async_copy(uest.at[y], ue.at[rows_of_me], ues.at[0]),
    ]
    for copies in u_moves[:8]:
        for copy in copies:
            copy.start()
    for copy in u_own:
        copy.start()

    for copy in k_moves[4:] + c_moves:
        copy.wait_recv()
    faces(5)

    for copy in ar1_moves:
        copy.wait_recv()
    arst[1] = jnp.max(ar1[...], axis=0)
    ar2[g] = arst[1]
    ar2_moves = [
        pltpu.make_async_remote_copy(
            src_ref=arst.at[1], dst_ref=ar2.at[g], send_sem=a2s.at[k], recv_sem=a2r.at[k],
            device_id=peer, device_id_type=MESH,
        )
        for k, peer in enumerate(along_g)
    ]
    for copy in ar2_moves:
        copy.start()
    for copy in ar2_moves:
        copy.wait_recv()
    bounds = jnp.max(jnp.max(ar2[...], axis=0), axis=1, keepdims=True)
    high = jnp.broadcast_to(bounds[0:1], (8, 128))
    low = -jnp.broadcast_to(bounds[4:5], (8, 128))
    theta = (high + low) / 2.0
    delta = (high - low) / 2.0
    sigma = theta / delta
    rho = 1.0 / sigma
    coefs[0] = 1.0 / theta
    for turn in range(LEVELS):
        rho_new = 1.0 / (2.0 * sigma - rho)
        coefs[1 + 2 * turn] = rho_new * rho
        coefs[2 + 2 * turn] = 2.0 * rho_new / delta * theta
        rho = rho_new

    def level(src, turn, q):
        lo, n = LO - q, B + 2 * q
        parts = 2 if n > 8 else 1
        c = n // parts
        inv, alpha, bet = coefs[0], coefs[1 + 2 * turn], coefs[2 + 2 * turn]
        before = src if turn == 0 else rb

        def row(i, _):
            for part in range(parts):
                j0 = lo + part * c
                at = pl.ds(j0, c)
                resid = before[i, at] - inv[None] * applied(src, i, j0, c)
                rb[i, at] = resid
                e[turn, i, at] = alpha[None] * src[i, at] + bet[None] * resid
            return 0
        lax.fori_loop(lo, lo + n, row, 0)

    def heat_step(start, q):
        src = start
        for turn in range(LEVELS):
            level(src, turn, q - 1 - turn)
            src = e.at[turn]

    def summed(start, i, at):
        total = start[i, at]
        for turn in range(LEVELS):
            total = total + e[turn, i, at]
        return xb[i, at] + coefs[0][None] * total

    for copy in v0_moves:
        copy.wait_recv()
    heat_step(v0, 6)

    for copy in x0_moves:
        copy.wait_send()

    def next_x(i, _):
        at = pl.ds(LO - 1, B + 2)
        xb[i, at] = summed(v0, i, at)
        return 0
    lax.fori_loop(LO - 1, HI + 1, next_x, 0)

    first_residual(xb, v1)
    v1_moves = halo(v1, 5, 4)
    for copy in v1_moves:
        copy.start()
    for copies in u_moves[8:]:
        for copy in copies:
            copy.start()
    for copy in v1_moves:
        copy.wait_recv()
    heat_step(v1, 5)

    def last_x(i, _):
        final = summed(v1, LO + i, pl.ds(LO, B))
        for j in range(B):
            ytr[i, pl.ds(j * 8, 8)] = final[j]
        return 0
    lax.fori_loop(0, B, last_x, 0)

    def to_natural(i, _):
        for kt in range(KT):
            natt[i, kt + 1] = ytr[i, pl.ds(kt, 8, stride=8), :]
        return 0
    lax.fori_loop(0, B, to_natural, 0)

    t_copies_out = [
        pltpu.make_async_copy(natt.at[:, kt + 1], t_out.at[:, :, pl.ds(kt * 128, 128)], osem.at[kt])
        for kt in range(KT)
    ]
    for copy in t_copies_out:
        copy.start()

    def pack_t(p, _):
        def one(i, edge):
            window, prev, nxt = pack(natt.at[i], p, i)
            tst[p, i] = window
            return jnp.where(lane == i, prev, jnp.where(lane == i + 32, nxt, edge))
        test[p] = lax.fori_loop(0, B, one, zero_tile)
        return 0
    lax.fori_loop(0, NY, pack_t, 0)

    def t_copies(k):
        p = lax.rem(y + k, NY)
        peer = (g, p)
        return [
            pltpu.make_async_remote_copy(
                src_ref=tst.at[p], dst_ref=t.at[pl.ds(1, B), rows_of_me],
                send_sem=ts.at[k], recv_sem=tr.at[k], device_id=peer, device_id_type=MESH,
            ),
            pltpu.make_async_remote_copy(
                src_ref=test.at[p], dst_ref=te.at[rows_of_me],
                send_sem=tes.at[k], recv_sem=ter.at[k], device_id=peer, device_id_type=MESH,
            ),
        ]

    t_moves = [t_copies(k) for k in range(1, NY)]
    t_own = [
        pltpu.make_async_copy(tst.at[y], t.at[pl.ds(1, B), rows_of_me], ts.at[0]),
        pltpu.make_async_copy(test.at[y], te.at[rows_of_me], tes.at[0]),
    ]
    for copies in t_moves:
        for copy in copies:
            copy.start()
    for copy in t_own:
        copy.start()

    for copy in u_own:
        copy.wait()
    for copies in u_moves:
        for copy in copies:
            copy.wait_recv()
    inner = pl.ds(8, 128)

    def plane_copies(buf, at, slot):
        return [
            pltpu.make_async_remote_copy(
                src_ref=buf.at[at(B)], dst_ref=buf.at[at(0)],
                send_sem=ps.at[slot, 0], recv_sem=pr.at[slot, 0], device_id=(gp, y), device_id_type=MESH,
            ),
            pltpu.make_async_remote_copy(
                src_ref=buf.at[at(1)], dst_ref=buf.at[at(B + 1)],
                send_sem=ps.at[slot, 1], recv_sem=pr.at[slot, 1], device_id=(gm, y), device_id_type=MESH,
            ),
        ]

    u_planes = plane_copies(u, lambda i: (slice(None), i, inner), 0)
    for copy in u_planes:
        copy.start()

    length = tally[y]
    wide_lane = lax.broadcasted_iota(jnp.int32, (128, 128), 1)
    valid = wide_lane < length

    def beside(own, edges, at):
        nxt = pltpu.roll(edges, (length - 1 - 32 - at + 256) & 127, 1)
        prev = pltpu.roll(edges, (128 - at) & 127, 1)
        plus = jnp.where(wide_lane == length - 1, nxt, pltpu.roll(own, 127, 1))
        minus = jnp.where(wide_lane == 0, prev, pltpu.roll(own, 1, 1))
        return plus, minus

    for copy in u_planes:
        copy.wait_recv()
    for a in range(3):
        u[a, 0, inner] = u[a, 0, inner] * inside_low_g
        u[a, B + 1, inner] = u[a, B + 1, inner] * inside_high_g

        def disp_row(i, _, a=a):
            own = u[a, i + 1, inner]
            plus, minus = beside(own, ue[inner], a * 8 + i)
            total = (
                u[a, i + 2, inner] + u[a, i, inner] + u[a, i + 1, pl.ds(9, 128)] + u[a, i + 1, pl.ds(7, 128)]
                + plus + minus
            )
            r_out[a, i] = mu[i] * (6.0 * own - total)
            return 0
        lax.fori_loop(0, B, disp_row, 0)

    for copy in t_own:
        copy.wait()
    for copies in t_moves:
        for copy in copies:
            copy.wait_recv()

    def stress_row(i, _):
        t[i + 1, inner] = beta[i] * t[i + 1, inner]
        return 0
    lax.fori_loop(0, B, stress_row, 0)
    t_planes = plane_copies(t, lambda i: (i, inner), 1)
    for copy in t_planes:
        copy.start()

    def stress_jk(i, _):
        own = t[i + 1, inner]
        plus, minus = beside(own, beta[i] * te[inner], i)
        along_j = t[i + 1, pl.ds(9, 128)] - t[i + 1, pl.ds(7, 128)]
        r_out[1, i] = jnp.where(valid, r_out[1, i] + 0.5 * along_j, 0.0)
        r_out[2, i] = jnp.where(valid, r_out[2, i] + 0.5 * (plus - minus), 0.0)
        return 0
    lax.fori_loop(0, B, stress_jk, 0)

    for copy in t_planes:
        copy.wait_recv()
    t[0, inner] = t[0, inner] * inside_low_g
    t[B + 1, inner] = t[B + 1, inner] * inside_high_g

    def stress_i(i, _):
        r_out[0, i] = jnp.where(valid, r_out[0, i] + 0.5 * (t[i + 2, inner] - t[i, inner]), 0.0)
        return 0
    lax.fori_loop(0, B, stress_i, 0)

    for copy in k_moves + c_moves + v0_moves + v1_moves + ar1_moves + ar2_moves + u_planes + t_planes:
        copy.wait_send()
    for copies in u_moves + t_moves:
        for copy in copies:
            copy.wait_send()
    for copy in t_copies_out:
        copy.wait()


def local(
    starting_warmth_level,
    diffusive_coefficient_map,
    specific_warmth_store,
    energy_source_flux,
    deformation_vector,
    substance_label_columns,
    substance_moduli_table,
    subdomain_point_tally,
):
    hbm = pl.BlockSpec(memory_space=pl.ANY)
    vmem = pl.BlockSpec(memory_space=pltpu.VMEM)
    smem = pl.BlockSpec(memory_space=pltpu.SMEM)
    grid = pltpu.VMEM((N, N, 8, 128), F32)
    dma = pltpu.SemaphoreType.DMA
    return pl.pallas_call(
        kernel,
        out_shape=(
            jax.ShapeDtypeStruct((B, B, KT * 128), F32),
            jax.ShapeDtypeStruct((3, B, NY * 8, ZMAX), F32),
        ),
        in_specs=[hbm] * 5 + [vmem, smem, smem],
        out_specs=(hbm, vmem),
        scratch_shapes=[
            pltpu.VMEM((4, B, KT * 8, 128), F32),
            pltpu.VMEM((3, B, KT + 2, 8, 128), F32),
            grid, grid, grid, grid, grid, grid,
            pltpu.VMEM((LEVELS, N, N, 8, 128), F32),
            grid, grid, grid, grid, grid,
            pltpu.VMEM((NY, 3, B, 8, 128), F32),
            pltpu.VMEM((NY, 8, 128), F32),
            pltpu.VMEM((3, B + 2, 8 + 128 + 8, 128), F32),
            pltpu.VMEM((8 + 128 + 8, 128), F32),
            pltpu.VMEM((NY, B, 8, 128), F32),
            pltpu.VMEM((NY, 8, 128), F32),
            pltpu.VMEM((B + 2, 8 + 128 + 8, 128), F32),
            pltpu.VMEM((8 + 128 + 8, 128), F32),
            pltpu.VMEM((B, KT + 2, 8, 128), F32),
            pltpu.VMEM((B, B * 8, 128), F32),
            pltpu.VMEM((B, 128, 128), F32),
            pltpu.VMEM((B, 128, 128), F32),
            pltpu.VMEM((NY, 8, 128), F32),
            pltpu.VMEM((NG, 8, 128), F32),
            pltpu.VMEM((2, 8, 128), F32),
            pltpu.VMEM((1 + 2 * LEVELS, 8, 128), F32),
            pltpu.SMEM((NY,), jnp.int32),
            dma((4, KT)), dma((KT,)),
            dma((5, 12)), dma((5, 12)),
            dma((NY - 1,)), dma((NY - 1,)), dma((NG - 1,)), dma((NG - 1,)),
            dma((NY,)), dma((NY,)), dma((NY,)), dma((NY,)),
            dma((NY,)), dma((NY,)), dma((NY,)), dma((NY,)),
            dma((2, 2)), dma((2, 2)),
            dma((KT,)),
        ],
        compiler_params=pltpu.CompilerParams(
            collective_id=0, has_side_effects=True, vmem_limit_bytes=58 * 2**20
        ),
    )(
        starting_warmth_level,
        diffusive_coefficient_map,
        specific_warmth_store,
        energy_source_flux,
        deformation_vector,
        substance_label_columns,
        substance_moduli_table,
        subdomain_point_tally,
    )


def solution(mesh):
    placed = (
        P("gx", "yz", None),
        P("gx", "yz", None),
        P("gx", "yz", None),
        P("gx", "yz", None),
        P(None, "gx", "yz", None),
        P("gx", None),
        P(),
        P(),
    )
    return jax.shard_map(
        local,
        mesh=mesh,
        in_specs=placed,
        out_specs=(P("gx", "yz", None), P(None, "gx", None, "yz")),
        check_vma=False,
    )
```

```python
import functools

import jax
import jax.numpy as jnp
from jax import lax
from jax.experimental import pallas as pl
from jax.experimental.pallas import tpu as pltpu
from jax.sharding import PartitionSpec as P

NCHEB = 6
ZMAX = 128
NG, NY = 8, 16
B = 8
H = 6
N = B + 2 * H
LO, HI = H, H + B
KT = 8
LEVELS = NCHEB - 1
MESH = pl.DeviceIdType.MESH
F32 = jnp.float32


def corner_rects(width):
    if width == 6:
        return [(1, 2, 5), (3, 5, 3)]
    if width == 5:
        return [(1, 2, 4), (3, 4, 2)]
    return []


def kernel(
    x0_hbm, k_hbm, c_hbm, f_hbm, u_hbm, lab, table, tally,
    t_out, r_out,
    nat, natu, kb, cb, xb, fb, v0, v1, e, rb, fx, fy, fz, db,
    ust, uest, u, ue, tst, t, natt, ytr,
    mu, beta, ar1, ar2, arst, coefs, starts,
    lsem, lusem, hs, hr, a1s, a1r, a2s, a2r, us, ur, ues, uer, ts, tr, ps, pr, bs, br, osem,
):
    g, y = lax.axis_index("gx"), lax.axis_index("yz")
    gp, gm = lax.rem(g + 1, NG), lax.rem(g + NG - 1, NG)
    yp, ym = lax.rem(y + 1, NY), lax.rem(y + NY - 1, NY)
    along_y = [(g, lax.rem(y + k, NY)) for k in range(1, NY)]
    along_g = [(lax.rem(g + k, NG), y) for k in range(1, NG)]
    core = lax.rem(g, 2)
    sibling = (g + 1 - 2 * core, y)
    across = lax.rem(g + 2 * core - 1 + NG, NG)
    diagonal = [(across, yp), (across, ym)]

    fields = [k_hbm, x0_hbm, c_hbm, f_hbm]
    own_in = [
        [
            pltpu.make_async_copy(
                field.at[:, :, pl.ds(kt * 128, 128)], nat.at[n, :, pl.ds(kt * 8, 8)], lsem.at[n, kt]
            )
            for kt in range(KT)
        ]
        for n, field in enumerate(fields)
    ]
    u_in = [
        pltpu.make_async_copy(
            u_hbm.at[:, :, :, pl.ds(kt * 128, 128)], natu.at[:, :, kt + 1], lusem.at[kt]
        )
        for kt in range(KT)
    ]
    for copies in own_in:
        for copy in copies:
            copy.start()
    for copy in u_in:
        copy.start()

    barrier = pltpu.get_barrier_semaphore()
    for peer in along_y + along_g + diagonal:
        pl.semaphore_signal(barrier, inc=1, device_id=peer, device_id_type=MESH)

    zero_tile = jnp.zeros((8, 128), F32)
    for a in range(3):
        def zero_u(i, _, a=a):
            u[a, i, pl.ds(0, 8)] = zero_tile
            u[a, i, pl.ds(8 + 128, 8)] = zero_tile
            return 0
        lax.fori_loop(0, B + 2, zero_u, 0)

        def zero_natu(i, _, a=a):
            natu[a, i, 0] = zero_tile
            natu[a, i, KT + 1] = zero_tile
            return 0
        lax.fori_loop(0, B, zero_natu, 0)

    def zero_t(i, _):
        t[i, pl.ds(0, 8)] = zero_tile
        t[i, pl.ds(8 + 128, 8)] = zero_tile
        return 0
    lax.fori_loop(0, B + 2, zero_t, 0)

    def zero_natt(i, _):
        natt[i, 0] = zero_tile
        natt[i, KT + 1] = zero_tile
        return 0
    lax.fori_loop(0, B + 2, zero_natt, 0)

    def to_lines(n, dst):
        def row(i, _):
            for j in range(B):
                dst[LO + i, LO + j] = nat[n, i, pl.ds(j, 8, stride=8), :]
            return 0
        lax.fori_loop(0, B, row, 0)

    for n, dst in ((0, kb), (1, xb), (2, cb), (3, fb)):
        for copy in own_in[n]:
            copy.wait()
        to_lines(n, dst)

    pl.semaphore_wait(barrier, len(along_y) + len(along_g) + len(diagonal))

    def halo(buf, width, slot, width_j=None):
        def sides(w):
            return pl.ds(LO - w, w), pl.ds(HI, w), pl.ds(LO, w), pl.ds(HI - w, w)

        own = pl.ds(LO, B)
        low_i, high_i, first_i, last_i = sides(width)
        low_j, high_j, first_j, last_j = sides(width_j or width)
        moves = [
            (buf.at[own, last_j], buf.at[own, low_j], (g, yp)),
            (buf.at[own, first_j], buf.at[own, high_j], (g, ym)),
            (buf.at[last_i, own], buf.at[low_i, own], (gp, y)),
            (buf.at[first_i, own], buf.at[high_i, own], (gm, y)),
        ]
        relayed = []
        for a0, a1, b1 in corner_rects(width):
            rows = a1 - a0 + 1
            in_low, out_low, in_high, out_high = LO + a0 - 1, LO - a1, HI - a1, HI - 1 + a0
            to_across, at_across = in_low + core * (in_high - in_low), out_high + core * (out_low - out_high)
            to_sibling, at_sibling = in_high + core * (in_low - in_high), out_low + core * (out_high - out_low)
            low, high, first, last = (pl.ds(LO - b1, b1), pl.ds(HI, b1), pl.ds(LO, b1), pl.ds(HI - b1, b1))
            src, dst = pl.ds(to_across, rows), pl.ds(at_across, rows)
            moves += [
                (buf.at[src, last], buf.at[dst, low], diagonal[0]),
                (buf.at[src, first], buf.at[dst, high], diagonal[1]),
            ]
            src, dst = pl.ds(to_sibling, rows), pl.ds(at_sibling, rows)
            relayed += [(buf.at[src, low], buf.at[dst, low], sibling), (buf.at[src, high], buf.at[dst, high], sibling)]
        copies = [
            pltpu.make_async_remote_copy(
                src_ref=src, dst_ref=dst, send_sem=hs.at[slot, m], recv_sem=hr.at[slot, m],
                device_id=peer, device_id_type=MESH,
            )
            for m, (src, dst, peer) in enumerate(moves + relayed)
        ]
        return copies[:len(moves)], copies[len(moves):]

    def relay(moves, relayed):
        for copy in moves[:2]:
            copy.wait_recv()
        for copy in relayed:
            copy.start()
        for copy in moves[2:] + relayed:
            copy.wait_recv()

    def plane_copies(buf, at, send, recv):
        return [
            pltpu.make_async_remote_copy(
                src_ref=buf.at[at(B)], dst_ref=buf.at[at(0)],
                send_sem=send.at[0], recv_sem=recv.at[0], device_id=(gp, y), device_id_type=MESH,
            ),
            pltpu.make_async_remote_copy(
                src_ref=buf.at[at(1)], dst_ref=buf.at[at(B + 1)],
                send_sem=send.at[1], recv_sem=recv.at[1], device_id=(gm, y), device_id_type=MESH,
            ),
        ]

    x0_moves, _ = halo(xb, 1, 0)
    k_moves, k_relayed = halo(kb, 6, 1)
    c_moves, c_relayed = halo(cb, 5, 2)
    for copy in x0_moves + k_moves + c_moves:
        copy.start()

    total = jnp.int32(0)
    for p in range(NY):
        starts[p] = total
        total = total + tally[p]

    eye = lax.broadcasted_iota(jnp.int32, (128, 128), 0) == lax.broadcasted_iota(jnp.int32, (128, 128), 1)

    def column_row(i, _):
        row = jnp.broadcast_to(lab[pl.ds(i, 1), :].astype(F32), (128, 128))
        column = jnp.sum(jnp.where(eye, row, 0.0), axis=1, keepdims=True)
        label = jnp.broadcast_to(column, (128, 128))
        for dst, r, at in ((mu, 0, i), (beta, 1, i + 1)):
            dst[at] = jnp.where(label == 0.0, table[r, 0], 0.0) + jnp.where(label == 1.0, table[r, 1], 0.0)
        return 0
    lax.fori_loop(0, B, column_row, 0)
    beta_planes = plane_copies(beta, lambda i: (i,), bs, br)
    for copy in beta_planes:
        copy.start()

    lane = lax.broadcasted_iota(jnp.int32, (8, 128), 1)

    def cuts(p):
        start = starts[p]
        before, after = start + 127, start + tally[p] + 128
        return (start >> 7) + 1, start & 127, before >> 7, before & 127, after >> 7, after & 127

    def pack(line, cut, lane_of, edge):
        tile, off, tile_before, lane_before, tile_after, lane_after = cut
        window = jnp.where(lane >= off, line[tile], line[tile + 1])
        prev = pltpu.roll(line[tile_before], (lane_of - lane_before + 256) & 127, 1)
        nxt = pltpu.roll(line[tile_after], (32 + lane_of - lane_after + 256) & 127, 1)
        edge = jnp.where(lane == lane_of, prev, jnp.where(lane == lane_of + 32, nxt, edge))
        return pltpu.roll(window, (128 - off) & 127, 1), edge

    for copy in u_in:
        copy.wait()

    def pack_u(p, _):
        cut = cuts(p)
        edge = zero_tile
        for a in range(3):
            for i in range(B):
                ust[p, a, i], edge = pack(natu.at[a, i], cut, a * 8 + i, edge)
        uest[p] = edge
        return 0
    lax.fori_loop(0, NY, pack_u, 0)

    rows_of_me = pl.ds(pl.multiple_of(8 + 8 * y, 8), 8)

    def u_copies(k):
        p = lax.rem(y + k, NY)
        peer = (g, p)
        return [
            pltpu.make_async_remote_copy(
                src_ref=ust.at[p], dst_ref=u.at[:, pl.ds(1, B), rows_of_me],
                send_sem=us.at[k], recv_sem=ur.at[k], device_id=peer, device_id_type=MESH,
            ),
            pltpu.make_async_remote_copy(
                src_ref=uest.at[p], dst_ref=ue.at[rows_of_me],
                send_sem=ues.at[k], recv_sem=uer.at[k], device_id=peer, device_id_type=MESH,
            ),
        ]

    u_moves = [u_copies(k) for k in range(1, NY)]
    u_own = [
        pltpu.make_async_copy(ust.at[y], u.at[:, pl.ds(1, B), rows_of_me], us.at[0]),
        pltpu.make_async_copy(uest.at[y], ue.at[rows_of_me], ues.at[0]),
    ]
    def send_u(ks):
        for k in ks:
            for copy in u_moves[k - 1]:
                copy.start()

    send_u((4, 8, 12))
    for copy in u_own:
        copy.start()

    def iota(n, axis):
        return lax.broadcasted_iota(jnp.int32, (n, 8, 128), axis)

    def up(v):
        by_lane = pltpu.roll(v, 127, 2)
        return jnp.where(iota(v.shape[0], 2) == 127, pltpu.roll(by_lane, 7, 1), by_lane)

    def down(v):
        by_lane = pltpu.roll(v, 1, 2)
        return jnp.where(iota(v.shape[0], 2) == 0, pltpu.roll(by_lane, 1, 1), by_lane)

    def harmonic(first, second):
        return 2.0 * first * second / (first + second)

    inside_low_g = jnp.where(g > 0, 1.0, 0.0)
    inside_high_g = jnp.where(g < NG - 1, 1.0, 0.0)
    inside_low_y = jnp.where(y > 0, 1.0, 0.0)
    inside_high_y = jnp.where(y < NY - 1, 1.0, 0.0)

    def faces(q):
        lo, n = LO - q, B + 2 * q

        whole = pl.ds(lo, n)
        fx[lo - 1, whole] = harmonic(kb[lo - 1, whole], kb[lo, whole])

        def fx_rows(step, _):
            i = lo + 2 * step
            low, high = harmonic(kb[i, whole], kb[i + 1, whole]), harmonic(kb[i + 1, whole], kb[i + 2, whole])
            fx[i, whole] = low
            fx[i + 1, whole] = high
            return 0
        lax.fori_loop(0, n // 2, fx_rows, 0)

        fx[LO - 1, pl.ds(lo, n)] = fx[LO - 1, pl.ds(lo, n)] * inside_low_g
        fx[HI - 1, pl.ds(lo, n)] = fx[HI - 1, pl.ds(lo, n)] * inside_high_g

        last = (iota(n, 1) == 7) & (iota(n, 2) == 127)

        def rows(step, _):
            first = lo + 2 * step
            done = []
            for i in (first, first + 1):
                own = kb[i, whole]
                low = harmonic(kb[i, lo - 1], kb[i, lo])
                along_j = harmonic(own, kb[i, pl.ds(lo + 1, n)])
                along_k = jnp.where(last, 0.0, harmonic(own, up(own)))
                done.append((low, along_j, along_k, cb[i, whole] + fx[i, whole] + fx[i - 1, whole] + along_k + down(along_k)))
            for i, (low, along_j, along_k, others) in enumerate(done):
                i = first + i
                fy[i, lo - 1] = low
                fy[i, whole] = along_j
                fz[i, whole] = along_k
                db[i, whole] = others
            return 0
        lax.fori_loop(0, n // 2, rows, 0)

        span = pl.ds(lo, n)
        fy[span, LO - 1] = fy[span, LO - 1] * inside_low_y
        fy[span, HI - 1] = fy[span, HI - 1] * inside_high_y

        def diagonal_row(i, _):
            db[i, whole] = db[i, whole] + fy[i, whole] + fy[i, pl.ds(lo - 1, n)]
            return 0
        lax.fori_loop(lo, lo + n, diagonal_row, 0)

    def applied(v, i, j0, c):
        at = pl.ds(j0, c)
        own, z = v[i, at], fz[i, at]
        return (
            db[i, at] * own
            - fx[i, at] * v[i + 1, at]
            - fx[i - 1, at] * v[i - 1, at]
            - fy[i, at] * v[i, pl.ds(j0 + 1, c)]
            - fy[i, pl.ds(j0 - 1, c)] * v[i, pl.ds(j0 - 1, c)]
            - z * up(own)
            - down(z * own)
        )

    def first_residual(x, dst):
        at = pl.ds(LO, B)
        done = [fb[i, at] + (cb[i, at] * x[i, at] - applied(x, i, LO, B)) for i in range(LO, HI)]
        for i, value in enumerate(done):
            dst[LO + i, at] = value

    for copy in x0_moves + k_moves[:4]:
        copy.wait_recv()
    for copy in k_relayed:
        copy.start()
    faces(0)

    def bound_row(i, carry):
        most, least = carry
        at = pl.ds(LO, B)
        c = cb[i, at]
        return (
            jnp.maximum(most, jnp.max(2.0 * db[i, at] - c, axis=0)),
            jnp.maximum(least, jnp.max(-c, axis=0)),
        )
    neg = jnp.full((8, 128), -3.0e38, F32)
    most, least = lax.fori_loop(LO, HI, bound_row, (neg, neg))
    sub = lax.broadcasted_iota(jnp.int32, (8, 128), 0)

    def over_rows(v):
        return jnp.broadcast_to(jnp.max(v, axis=0, keepdims=True), (8, 128))

    arst[0] = jnp.where(sub < 4, over_rows(most), over_rows(least))
    ar1[y] = arst[0]
    ar1_moves = [
        pltpu.make_async_remote_copy(
            src_ref=arst.at[0], dst_ref=ar1.at[y], send_sem=a1s.at[k], recv_sem=a1r.at[k],
            device_id=peer, device_id_type=MESH,
        )
        for k, peer in enumerate(along_y)
    ]
    for copy in ar1_moves:
        copy.start()

    first_residual(xb, v0)
    v0_moves, v0_relayed = halo(v0, 6, 3)
    for copy in v0_moves:
        copy.start()

    relay(c_moves, c_relayed)
    for copy in k_moves[4:] + k_relayed:
        copy.wait_recv()
    faces(5)

    for copy in ar1_moves:
        copy.wait_recv()
    arst[1] = jnp.max(ar1[...], axis=0)
    ar2[g] = arst[1]
    ar2_moves = [
        pltpu.make_async_remote_copy(
            src_ref=arst.at[1], dst_ref=ar2.at[g], send_sem=a2s.at[k], recv_sem=a2r.at[k],
            device_id=peer, device_id_type=MESH,
        )
        for k, peer in enumerate(along_g)
    ]
    for copy in ar2_moves:
        copy.start()
    for copy in ar2_moves:
        copy.wait_recv()
    bounds = jnp.max(jnp.max(ar2[...], axis=0), axis=1, keepdims=True)
    high = jnp.broadcast_to(bounds[0:1], (8, 128))
    low = -jnp.broadcast_to(bounds[4:5], (8, 128))
    theta = (high + low) / 2.0
    delta = (high - low) / 2.0
    sigma = theta / delta
    rho = 1.0 / sigma
    coefs[0] = 1.0 / theta
    for turn in range(LEVELS):
        rho_new = 1.0 / (2.0 * sigma - rho)
        coefs[1 + 2 * turn] = rho_new * rho
        coefs[2 + 2 * turn] = 2.0 * rho_new / delta * theta
        rho = rho_new

    def level(src, turn, qi, qj):
        lo, n = LO - qi, B + 2 * qi
        rows = max(d for d in range(1, 10) if n % d == 0)
        j0, c = LO - qj, B + 2 * qj
        at = pl.ds(j0, c)
        inv, alpha, bet = coefs[0], coefs[1 + 2 * turn], coefs[2 + 2 * turn]
        before = src if turn == 0 else rb

        def some_rows(step, _):
            first = lo + step * rows
            done = []
            for i in range(rows):
                resid = before[first + i, at] - inv[None] * applied(src, first + i, j0, c)
                done.append((resid, alpha[None] * src[first + i, at] + bet[None] * resid))
            for i, (resid, value) in enumerate(done):
                rb[first + i, at] = resid
                e[turn, first + i, at] = value
            return 0
        lax.fori_loop(0, n // rows, some_rows, 0)

    def heat_step(start, qi, qj):
        src = start
        for turn in range(LEVELS):
            level(src, turn, qi - 1 - turn, qj - 1 - turn)
            src = e.at[turn]

    def summed(start, i, at):
        total = start[i, at]
        for turn in range(LEVELS):
            total = total + e[turn, i, at]
        return xb[i, at] + coefs[0][None] * total

    relay(v0_moves, v0_relayed)
    send_u((1, 3, 5, 7, 9, 11))
    heat_step(v0, 6, 6)

    for copy in x0_moves:
        copy.wait_send()

    def next_x(i, _):
        at = pl.ds(LO - 1, B + 2)
        xb[i, at] = summed(v0, i, at)
        return 0
    lax.fori_loop(LO - 1, HI + 1, next_x, 0)

    first_residual(xb, v1)
    v1_moves, v1_relayed = halo(v1, 6, 4, 5)
    for copy in v1_moves:
        copy.start()
    send_u((13, 15, 2, 6, 10, 14))
    relay(v1_moves, v1_relayed)
    heat_step(v1, 6, 5)

    def last_x(i, _):
        final = summed(v1, LO - 1 + i, pl.ds(LO, B))
        for j in range(B):
            ytr[i, pl.ds(j * 8, 8)] = final[j]
        return 0
    lax.fori_loop(0, B + 2, last_x, 0)

    def to_natural(i, _):
        for kt in range(KT):
            natt[i, kt + 1] = ytr[i, pl.ds(kt, 8, stride=8), :]
        return 0
    lax.fori_loop(0, B + 2, to_natural, 0)

    t_copies_out = [
        pltpu.make_async_copy(natt.at[pl.ds(1, B), kt + 1], t_out.at[:, :, pl.ds(kt * 128, 128)], osem.at[kt])
        for kt in range(KT)
    ]
    for copy in t_copies_out:
        copy.start()

    def t_copies(k):
        p = lax.rem(y + k, NY)
        peer = (g, p)
        return [
            pltpu.make_async_remote_copy(
                src_ref=tst.at[p], dst_ref=t.at[:, rows_of_me],
                send_sem=ts.at[k], recv_sem=tr.at[k], device_id=peer, device_id_type=MESH,
            )
        ]

    t_moves = [t_copies(k) for k in range(1, NY)]
    t_own = [
        pltpu.make_async_copy(tst.at[y], t.at[:, rows_of_me], ts.at[0]),
    ]
    for group in ((10, 6, 9, 11), (14, 2, 5, 7), (13, 15, 8, 3), (1, 4, 12, 0)):
        done = []
        for k in group:
            p = lax.rem(y + k, NY)
            cut = cuts(p)
            edge = zero_tile
            windows = []
            for i in range(B + 2):
                window, edge = pack(natt.at[i], cut, i, edge)
                windows.append(window)
            done.append((k, p, windows + [edge]))
        for k, p, windows in done:
            for i, window in enumerate(windows):
                tst[p, i] = window
            for copy in t_own if k == 0 else t_moves[k - 1]:
                copy.start()

    for copy in u_own:
        copy.wait()
    for copies in u_moves:
        for copy in copies:
            copy.wait_recv()
    inner = pl.ds(8, 128)

    u_planes = plane_copies(u, lambda i: (slice(None), i, inner), ps, pr)
    for copy in u_planes:
        copy.start()

    length = tally[y]
    wide_lane = lax.broadcasted_iota(jnp.int32, (128, 128), 1)
    valid = wide_lane < length

    def beside(own, edges, at):
        nxt = pltpu.roll(edges, (length - 1 - 32 - at + 256) & 127, 1)
        prev = pltpu.roll(edges, (128 - at) & 127, 1)
        plus = jnp.where(wide_lane == length - 1, nxt, pltpu.roll(own, 127, 1))
        minus = jnp.where(wide_lane == 0, prev, pltpu.roll(own, 1, 1))
        return plus, minus

    for copy in u_planes:
        copy.wait_recv()
    for a in range(3):
        u[a, 0, inner] = u[a, 0, inner] * inside_low_g
        u[a, B + 1, inner] = u[a, B + 1, inner] * inside_high_g

        def disp_row(i, _, a=a):
            own = u[a, i + 1, inner]
            plus, minus = beside(own, ue[inner], a * 8 + i)
            total = (
                u[a, i + 2, inner] + u[a, i, inner] + u[a, i + 1, pl.ds(9, 128)] + u[a, i + 1, pl.ds(7, 128)]
                + plus + minus
            )
            r_out[a, i] = mu[i] * (6.0 * own - total)
            return 0
        lax.fori_loop(0, B, disp_row, 0)

    for copy in t_own:
        copy.wait()
    for copies in t_moves:
        for copy in copies:
            copy.wait_recv()

    for copy in beta_planes:
        copy.wait_recv()
    beta[0] = beta[0] * inside_low_g
    beta[B + 1] = beta[B + 1] * inside_high_g

    def stress_row(i, _):
        t[i, inner] = beta[i] * t[i, inner]
        return 0
    lax.fori_loop(0, B + 2, stress_row, 0)

    def stress_part(i, _):
        plus, minus = beside(t[i + 1, inner], beta[i + 1] * t[B + 2, inner], i + 1)
        along_i = t[i + 2, inner] - t[i, inner]
        along_j = t[i + 1, pl.ds(9, 128)] - t[i + 1, pl.ds(7, 128)]
        r_out[0, i] = jnp.where(valid, r_out[0, i] + 0.5 * along_i, 0.0)
        r_out[1, i] = jnp.where(valid, r_out[1, i] + 0.5 * along_j, 0.0)
        r_out[2, i] = jnp.where(valid, r_out[2, i] + 0.5 * (plus - minus), 0.0)
        return 0
    lax.fori_loop(0, B, stress_part, 0)

    for copy in k_moves + k_relayed + c_moves + c_relayed + v0_moves + v0_relayed + v1_moves + v1_relayed:
        copy.wait_send()
    for copy in ar1_moves + ar2_moves + u_planes + beta_planes:
        copy.wait_send()
    for copies in u_moves + t_moves:
        for copy in copies:
            copy.wait_send()
    for copy in t_copies_out:
        copy.wait()


def local(
    starting_warmth_level,
    diffusive_coefficient_map,
    specific_warmth_store,
    energy_source_flux,
    deformation_vector,
    substance_label_columns,
    substance_moduli_table,
    subdomain_point_tally,
):
    hbm = pl.BlockSpec(memory_space=pl.ANY)
    vmem = pl.BlockSpec(memory_space=pltpu.VMEM)
    smem = pl.BlockSpec(memory_space=pltpu.SMEM)
    grid = pltpu.VMEM((N, N, 8, 128), F32)
    dma = pltpu.SemaphoreType.DMA
    return pl.pallas_call(
        kernel,
        out_shape=(
            jax.ShapeDtypeStruct((B, B, KT * 128), F32),
            jax.ShapeDtypeStruct((3, B, NY * 8, ZMAX), F32),
        ),
        in_specs=[hbm] * 5 + [vmem, smem, smem],
        out_specs=(hbm, vmem),
        scratch_shapes=[
            pltpu.VMEM((4, B, KT * 8, 128), F32),
            pltpu.VMEM((3, B, KT + 2, 8, 128), F32),
            grid, grid, grid, grid, grid, grid,
            pltpu.VMEM((LEVELS, N, N, 8, 128), F32),
            grid, grid, grid, grid, grid,
            pltpu.VMEM((NY, 3, B, 8, 128), F32),
            pltpu.VMEM((NY, 8, 128), F32),
            pltpu.VMEM((3, B + 2, 8 + 128 + 8, 128), F32),
            pltpu.VMEM((8 + 128 + 8, 128), F32),
            pltpu.VMEM((NY, B + 3, 8, 128), F32),
            pltpu.VMEM((B + 3, 8 + 128 + 8, 128), F32),
            pltpu.VMEM((B + 2, KT + 2, 8, 128), F32),
            pltpu.VMEM((B + 2, B * 8, 128), F32),
            pltpu.VMEM((B, 128, 128), F32),
            pltpu.VMEM((B + 2, 128, 128), F32),
            pltpu.VMEM((NY, 8, 128), F32),
            pltpu.VMEM((NG, 8, 128), F32),
            pltpu.VMEM((2, 8, 128), F32),
            pltpu.VMEM((1 + 2 * LEVELS, 8, 128), F32),
            pltpu.SMEM((NY,), jnp.int32),
            dma((4, KT)), dma((KT,)),
            dma((5, 12)), dma((5, 12)),
            dma((NY - 1,)), dma((NY - 1,)), dma((NG - 1,)), dma((NG - 1,)),
            dma((NY,)), dma((NY,)), dma((NY,)), dma((NY,)),
            dma((NY,)), dma((NY,)),
            dma((2,)), dma((2,)), dma((2,)), dma((2,)),
            dma((KT,)),
        ],
        compiler_params=pltpu.CompilerParams(
            collective_id=0, has_side_effects=True, vmem_limit_bytes=58 * 2**20
        ),
    )(
        starting_warmth_level,
        diffusive_coefficient_map,
        specific_warmth_store,
        energy_source_flux,
        deformation_vector,
        substance_label_columns,
        substance_moduli_table,
        subdomain_point_tally,
    )


def solution(mesh):
    placed = (
        P("gx", "yz", None),
        P("gx", "yz", None),
        P("gx", "yz", None),
        P("gx", "yz", None),
        P(None, "gx", "yz", None),
        P("gx", None),
        P(),
        P(),
    )
    return jax.shard_map(
        local,
        mesh=mesh,
        in_specs=placed,
        out_specs=(P("gx", "yz", None), P(None, "gx", None, "yz")),
        check_vma=False,
    )
```

```python
import functools

import jax
import jax.numpy as jnp
from jax import lax
from jax.experimental import pallas as pl
from jax.experimental.pallas import tpu as pltpu
from jax.sharding import PartitionSpec as P

NCHEB = 6
ZMAX = 128
NG, NY = 8, 16
B = 8
H = 6
N = B + 2 * H
LO, HI = H, H + B
KT = 8
LEVELS = NCHEB - 1
MESH = pl.DeviceIdType.MESH
F32 = jnp.float32


def corner_rects(width):
    if width == 6:
        return [(1, 2, 5), (3, 5, 3)]
    if width == 5:
        return [(1, 2, 4), (3, 4, 2)]
    return []


def kernel(
    x0_hbm, k_hbm, c_hbm, f_hbm, u_hbm, lab, table, tally,
    t_out, r_out,
    nat, natu, kb, cb, xb, fb, v0, v1, e, rb, fx, fy, fz, db,
    ust, uest, u, ue, tst, t, natt, ytr,
    mu, beta, ar1, ar2, arst, coefs, starts,
    lsem, lusem, hs, hr, a1s, a1r, a2s, a2r, us, ur, ues, uer, ts, tr, ps, pr, bs, br,
):
    g, y = lax.axis_index("gx"), lax.axis_index("yz")
    gp, gm = lax.rem(g + 1, NG), lax.rem(g + NG - 1, NG)
    yp, ym = lax.rem(y + 1, NY), lax.rem(y + NY - 1, NY)
    along_y = [(g, lax.rem(y + k, NY)) for k in range(1, NY)]
    along_g = [(lax.rem(g + k, NG), y) for k in range(1, NG)]
    core = lax.rem(g, 2)
    sibling = (g + 1 - 2 * core, y)
    across = lax.rem(g + 2 * core - 1 + NG, NG)
    diagonal = [(across, yp), (across, ym)]

    fields = [k_hbm, x0_hbm, c_hbm, f_hbm]
    own_in = [
        [
            pltpu.make_async_copy(
                field.at[:, :, pl.ds(kt * 128, 128)], nat.at[n, :, pl.ds(kt * 8, 8)], lsem.at[n, kt]
            )
            for kt in range(KT)
        ]
        for n, field in enumerate(fields)
    ]
    u_in = [
        pltpu.make_async_copy(
            u_hbm.at[:, :, :, pl.ds(kt * 128, 128)], natu.at[:, :, kt + 1], lusem.at[kt]
        )
        for kt in range(KT)
    ]
    for copies in own_in:
        for copy in copies:
            copy.start()
    for copy in u_in:
        copy.start()

    barrier = pltpu.get_barrier_semaphore()
    for peer in along_y + along_g + diagonal:
        pl.semaphore_signal(barrier, inc=1, device_id=peer, device_id_type=MESH)

    zero_tile = jnp.zeros((8, 128), F32)
    for a in range(3):
        def zero_u(i, _, a=a):
            u[a, i, pl.ds(0, 8)] = zero_tile
            u[a, i, pl.ds(8 + 128, 8)] = zero_tile
            return 0
        lax.fori_loop(0, B + 2, zero_u, 0)

        def zero_natu(i, _, a=a):
            natu[a, i, 0] = zero_tile
            natu[a, i, KT + 1] = zero_tile
            return 0
        lax.fori_loop(0, B, zero_natu, 0)

    def zero_t(i, _):
        t[i, pl.ds(0, 8)] = zero_tile
        t[i, pl.ds(8 + 128, 8)] = zero_tile
        return 0
    lax.fori_loop(0, B + 2, zero_t, 0)

    def zero_natt(i, _):
        natt[i, 0] = zero_tile
        natt[i, KT + 1] = zero_tile
        return 0
    lax.fori_loop(0, B + 2, zero_natt, 0)

    def to_lines(n, dst):
        def row(i, _):
            for j in range(B):
                dst[LO + i, LO + j] = nat[n, i, pl.ds(j, 8, stride=8), :]
            return 0
        lax.fori_loop(0, B, row, 0)

    for n, dst in ((0, kb), (1, xb), (2, cb), (3, fb)):
        for copy in own_in[n]:
            copy.wait()
        to_lines(n, dst)

    pl.semaphore_wait(barrier, len(along_y) + len(along_g) + len(diagonal))

    def halo(buf, width, slot, width_j=None):
        def sides(w):
            return pl.ds(LO - w, w), pl.ds(HI, w), pl.ds(LO, w), pl.ds(HI - w, w)

        own = pl.ds(LO, B)
        low_i, high_i, first_i, last_i = sides(width)
        low_j, high_j, first_j, last_j = sides(width_j or width)
        moves = [
            (buf.at[own, last_j], buf.at[own, low_j], (g, yp)),
            (buf.at[own, first_j], buf.at[own, high_j], (g, ym)),
            (buf.at[last_i, own], buf.at[low_i, own], (gp, y)),
            (buf.at[first_i, own], buf.at[high_i, own], (gm, y)),
        ]
        relayed = []
        for a0, a1, b1 in corner_rects(width):
            rows = a1 - a0 + 1
            in_low, out_low, in_high, out_high = LO + a0 - 1, LO - a1, HI - a1, HI - 1 + a0
            to_across, at_across = in_low + core * (in_high - in_low), out_high + core * (out_low - out_high)
            to_sibling, at_sibling = in_high + core * (in_low - in_high), out_low + core * (out_high - out_low)
            low, high, first, last = (pl.ds(LO - b1, b1), pl.ds(HI, b1), pl.ds(LO, b1), pl.ds(HI - b1, b1))
            src, dst = pl.ds(to_across, rows), pl.ds(at_across, rows)
            moves += [
                (buf.at[src, last], buf.at[dst, low], diagonal[0]),
                (buf.at[src, first], buf.at[dst, high], diagonal[1]),
            ]
            src, dst = pl.ds(to_sibling, rows), pl.ds(at_sibling, rows)
            relayed += [(buf.at[src, low], buf.at[dst, low], sibling), (buf.at[src, high], buf.at[dst, high], sibling)]
        copies = [
            pltpu.make_async_remote_copy(
                src_ref=src, dst_ref=dst, send_sem=hs.at[slot, m], recv_sem=hr.at[slot, m],
                device_id=peer, device_id_type=MESH,
            )
            for m, (src, dst, peer) in enumerate(moves + relayed)
        ]
        return copies[:len(moves)], copies[len(moves):]

    def relay_start(moves, relayed):
        for copy in moves[:2]:
            copy.wait_recv()
        for copy in relayed:
            copy.start()

    def relay(moves, relayed):
        relay_start(moves, relayed)
        for copy in moves[2:] + relayed:
            copy.wait_recv()

    def plane_copies(buf, at, send, recv):
        return [
            pltpu.make_async_remote_copy(
                src_ref=buf.at[at(B)], dst_ref=buf.at[at(0)],
                send_sem=send.at[0], recv_sem=recv.at[0], device_id=(gp, y), device_id_type=MESH,
            ),
            pltpu.make_async_remote_copy(
                src_ref=buf.at[at(1)], dst_ref=buf.at[at(B + 1)],
                send_sem=send.at[1], recv_sem=recv.at[1], device_id=(gm, y), device_id_type=MESH,
            ),
        ]

    x0_moves, _ = halo(xb, 1, 0)
    k_moves, k_relayed = halo(kb, 6, 1)
    c_moves, c_relayed = halo(cb, 5, 2)
    for copy in x0_moves + k_moves + c_moves:
        copy.start()

    total = jnp.int32(0)
    for p in range(NY):
        starts[p] = total
        total = total + tally[p]

    eye = lax.broadcasted_iota(jnp.int32, (128, 128), 0) == lax.broadcasted_iota(jnp.int32, (128, 128), 1)

    def column_row(i, _):
        row = jnp.broadcast_to(lab[pl.ds(i, 1), :].astype(F32), (128, 128))
        column = jnp.sum(jnp.where(eye, row, 0.0), axis=1, keepdims=True)
        label = jnp.broadcast_to(column, (128, 128))
        for dst, r, at in ((mu, 0, i), (beta, 1, i + 1)):
            dst[at] = jnp.where(label == 0.0, table[r, 0], 0.0) + jnp.where(label == 1.0, table[r, 1], 0.0)
        return 0
    lax.fori_loop(0, B, column_row, 0)
    beta_planes = plane_copies(beta, lambda i: (i,), bs, br)
    for copy in beta_planes:
        copy.start()

    lane = lax.broadcasted_iota(jnp.int32, (8, 128), 1)

    def cuts(p):
        start = starts[p]
        before, after = start + 127, start + tally[p] + 128
        return (start >> 7) + 1, start & 127, before >> 7, before & 127, after >> 7, after & 127

    def pack(line, cut, lane_of, edge):
        tile, off, tile_before, lane_before, tile_after, lane_after = cut
        window = jnp.where(lane >= off, line[tile], line[tile + 1])
        prev = pltpu.roll(line[tile_before], (lane_of - lane_before + 256) & 127, 1)
        nxt = pltpu.roll(line[tile_after], (32 + lane_of - lane_after + 256) & 127, 1)
        edge = jnp.where(lane == lane_of, prev, jnp.where(lane == lane_of + 32, nxt, edge))
        return pltpu.roll(window, (128 - off) & 127, 1), edge

    for copy in u_in:
        copy.wait()

    def pack_u(p, _):
        cut = cuts(p)
        edge = zero_tile
        for a in range(3):
            for i in range(B):
                ust[p, a, i], edge = pack(natu.at[a, i], cut, a * 8 + i, edge)
        uest[p] = edge
        return 0
    lax.fori_loop(0, NY, pack_u, 0)

    rows_of_me = pl.ds(pl.multiple_of(8 + 8 * y, 8), 8)

    def u_copies(k):
        p = lax.rem(y + k, NY)
        peer = (g, p)
        return [
            pltpu.make_async_remote_copy(
                src_ref=ust.at[p], dst_ref=u.at[:, pl.ds(1, B), rows_of_me],
                send_sem=us.at[k], recv_sem=ur.at[k], device_id=peer, device_id_type=MESH,
            ),
            pltpu.make_async_remote_copy(
                src_ref=uest.at[p], dst_ref=ue.at[rows_of_me],
                send_sem=ues.at[k], recv_sem=uer.at[k], device_id=peer, device_id_type=MESH,
            ),
        ]

    u_moves = [u_copies(k) for k in range(1, NY)]
    u_own = [
        pltpu.make_async_copy(ust.at[y], u.at[:, pl.ds(1, B), rows_of_me], us.at[0]),
        pltpu.make_async_copy(uest.at[y], ue.at[rows_of_me], ues.at[0]),
    ]
    def send_u(ks):
        for k in ks:
            for copy in u_moves[k - 1]:
                copy.start()

    send_u((4, 8, 12))
    for copy in u_own:
        copy.start()

    def iota(n, axis):
        return lax.broadcasted_iota(jnp.int32, (n, 8, 128), axis)

    def up(v):
        by_lane = pltpu.roll(v, 127, 2)
        return jnp.where(iota(v.shape[0], 2) == 127, pltpu.roll(by_lane, 7, 1), by_lane)

    def down(v):
        by_lane = pltpu.roll(v, 1, 2)
        return jnp.where(iota(v.shape[0], 2) == 0, pltpu.roll(by_lane, 1, 1), by_lane)

    def harmonic(first, second):
        return 2.0 * first * second / (first + second)

    inside_low_g = jnp.where(g > 0, 1.0, 0.0)
    inside_high_g = jnp.where(g < NG - 1, 1.0, 0.0)
    inside_low_y = jnp.where(y > 0, 1.0, 0.0)
    inside_high_y = jnp.where(y < NY - 1, 1.0, 0.0)

    def faces(q):
        lo, n = LO - q, B + 2 * q

        whole = pl.ds(lo, n)
        fx[lo - 1, whole] = harmonic(kb[lo - 1, whole], kb[lo, whole])

        def fx_rows(step, _):
            i = lo + 2 * step
            low, high = harmonic(kb[i, whole], kb[i + 1, whole]), harmonic(kb[i + 1, whole], kb[i + 2, whole])
            fx[i, whole] = low
            fx[i + 1, whole] = high
            return 0
        lax.fori_loop(0, n // 2, fx_rows, 0)

        fx[LO - 1, pl.ds(lo, n)] = fx[LO - 1, pl.ds(lo, n)] * inside_low_g
        fx[HI - 1, pl.ds(lo, n)] = fx[HI - 1, pl.ds(lo, n)] * inside_high_g

        last = (iota(n, 1) == 7) & (iota(n, 2) == 127)

        def rows(step, _):
            first = lo + 2 * step
            done = []
            for i in (first, first + 1):
                own = kb[i, whole]
                low = harmonic(kb[i, lo - 1], kb[i, lo])
                along_j = harmonic(own, kb[i, pl.ds(lo + 1, n)])
                along_k = jnp.where(last, 0.0, harmonic(own, up(own)))
                done.append((low, along_j, along_k, cb[i, whole] + fx[i, whole] + fx[i - 1, whole] + along_k + down(along_k)))
            for i, (low, along_j, along_k, others) in enumerate(done):
                i = first + i
                fy[i, lo - 1] = low
                fy[i, whole] = along_j
                fz[i, whole] = along_k
                db[i, whole] = others
            return 0
        lax.fori_loop(0, n // 2, rows, 0)

        span = pl.ds(lo, n)
        fy[span, LO - 1] = fy[span, LO - 1] * inside_low_y
        fy[span, HI - 1] = fy[span, HI - 1] * inside_high_y

        def diagonal_row(i, _):
            db[i, whole] = db[i, whole] + fy[i, whole] + fy[i, pl.ds(lo - 1, n)]
            return 0
        lax.fori_loop(lo, lo + n, diagonal_row, 0)

    def applied(v, i, j0, c):
        at = pl.ds(j0, c)
        own, z = v[i, at], fz[i, at]
        return (
            db[i, at] * own
            - fx[i, at] * v[i + 1, at]
            - fx[i - 1, at] * v[i - 1, at]
            - fy[i, at] * v[i, pl.ds(j0 + 1, c)]
            - fy[i, pl.ds(j0 - 1, c)] * v[i, pl.ds(j0 - 1, c)]
            - z * up(own)
            - down(z * own)
        )

    def first_residual(x, dst):
        at = pl.ds(LO, B)
        done = [fb[i, at] + (cb[i, at] * x[i, at] - applied(x, i, LO, B)) for i in range(LO, HI)]
        for i, value in enumerate(done):
            dst[LO + i, at] = value

    for copy in x0_moves + k_moves[:4]:
        copy.wait_recv()
    for copy in k_relayed:
        copy.start()
    faces(0)

    def bound_row(i, carry):
        most, least = carry
        at = pl.ds(LO, B)
        c = cb[i, at]
        return (
            jnp.maximum(most, jnp.max(2.0 * db[i, at] - c, axis=0)),
            jnp.maximum(least, jnp.max(-c, axis=0)),
        )
    neg = jnp.full((8, 128), -3.0e38, F32)
    most, least = lax.fori_loop(LO, HI, bound_row, (neg, neg))
    sub = lax.broadcasted_iota(jnp.int32, (8, 128), 0)

    def over_rows(v):
        return jnp.broadcast_to(jnp.max(v, axis=0, keepdims=True), (8, 128))

    arst[0] = jnp.where(sub < 4, over_rows(most), over_rows(least))
    ar1[y] = arst[0]
    ar1_moves = [
        pltpu.make_async_remote_copy(
            src_ref=arst.at[0], dst_ref=ar1.at[y], send_sem=a1s.at[k], recv_sem=a1r.at[k],
            device_id=peer, device_id_type=MESH,
        )
        for k, peer in enumerate(along_y)
    ]
    for copy in ar1_moves:
        copy.start()

    first_residual(xb, v0)
    v0_moves, v0_relayed = halo(v0, 6, 3)
    for copy in v0_moves:
        copy.start()

    send_u((1, 3, 5, 7, 9, 11))
    relay_start(c_moves, c_relayed)
    for copy in ar1_moves:
        copy.wait_recv()
    arst[1] = jnp.max(ar1[...], axis=0)
    ar2[g] = arst[1]
    ar2_moves = [
        pltpu.make_async_remote_copy(
            src_ref=arst.at[1], dst_ref=ar2.at[g], send_sem=a2s.at[k], recv_sem=a2r.at[k],
            device_id=peer, device_id_type=MESH,
        )
        for k, peer in enumerate(along_g)
    ]
    for copy in ar2_moves:
        copy.start()
    for copy in c_moves[2:] + c_relayed + k_moves[4:] + k_relayed:
        copy.wait_recv()
    faces(5)

    for copy in ar2_moves:
        copy.wait_recv()
    send_u((13, 15, 2, 6, 10, 14))
    for copy in beta_planes:
        copy.wait()
    beta[0] = beta[0] * inside_low_g
    beta[B + 1] = beta[B + 1] * inside_high_g

    bounds = jnp.max(jnp.max(ar2[...], axis=0), axis=1, keepdims=True)
    high = jnp.broadcast_to(bounds[0:1], (8, 128))
    low = -jnp.broadcast_to(bounds[4:5], (8, 128))
    theta = (high + low) / 2.0
    delta = (high - low) / 2.0
    sigma = theta / delta
    rho = 1.0 / sigma
    coefs[0] = 1.0 / theta
    for turn in range(LEVELS):
        rho_new = 1.0 / (2.0 * sigma - rho)
        coefs[1 + 2 * turn] = rho_new * rho
        coefs[2 + 2 * turn] = 2.0 * rho_new / delta * theta
        rho = rho_new

    def level(src, turn, qi, qj):
        lo, n = LO - qi, B + 2 * qi
        rows = max(d for d in range(1, 10) if n % d == 0)
        j0, c = LO - qj, B + 2 * qj
        at = pl.ds(j0, c)
        inv, alpha, bet = coefs[0], coefs[1 + 2 * turn], coefs[2 + 2 * turn]
        before = src if turn == 0 else rb

        def some_rows(step, _):
            first = lo + step * rows
            done = []
            for i in range(rows):
                resid = before[first + i, at] - inv[None] * applied(src, first + i, j0, c)
                done.append((resid, alpha[None] * src[first + i, at] + bet[None] * resid))
            for i, (resid, value) in enumerate(done):
                rb[first + i, at] = resid
                e[turn, first + i, at] = value
            return 0
        lax.fori_loop(0, n // rows, some_rows, 0)

    def heat_step(start, qi, qj):
        src = start
        for turn in range(LEVELS):
            level(src, turn, qi - 1 - turn, qj - 1 - turn)
            src = e.at[turn]

    def summed(start, i, at):
        total = start[i, at]
        for turn in range(LEVELS):
            total = total + e[turn, i, at]
        return xb[i, at] + coefs[0][None] * total

    relay(v0_moves, v0_relayed)
    heat_step(v0, 6, 6)

    for copy in x0_moves:
        copy.wait_send()

    def next_x(i, _):
        at = pl.ds(LO - 1, B + 2)
        xb[i, at] = summed(v0, i, at)
        return 0
    lax.fori_loop(LO - 1, HI + 1, next_x, 0)

    first_residual(xb, v1)
    v1_moves, v1_relayed = halo(v1, 6, 4, 5)
    for copy in v1_moves:
        copy.start()
    relay(v1_moves, v1_relayed)
    heat_step(v1, 6, 5)

    def last_x(i, _):
        final = summed(v1, LO - 1 + i, pl.ds(LO, B))
        for j in range(B):
            ytr[i, pl.ds(j * 8, 8)] = final[j]
        return 0
    lax.fori_loop(0, B + 2, last_x, 0)

    def to_natural(i, _):
        for kt in range(KT):
            natt[i, kt + 1] = ytr[i, pl.ds(kt, 8, stride=8), :]
        return 0
    lax.fori_loop(0, B + 2, to_natural, 0)

    for kt in range(KT):
        t_out[:, :, pl.ds(kt * 128, 128)] = natt[pl.ds(1, B), kt + 1]

    def t_copies(k):
        p = lax.rem(y + k, NY)
        peer = (g, p)
        return [
            pltpu.make_async_remote_copy(
                src_ref=tst.at[p], dst_ref=t.at[:, rows_of_me],
                send_sem=ts.at[k], recv_sem=tr.at[k], device_id=peer, device_id_type=MESH,
            )
        ]

    t_moves = [t_copies(k) for k in range(1, NY)]
    t_own = [
        pltpu.make_async_copy(tst.at[y], t.at[:, rows_of_me], ts.at[0]),
    ]
    for group in ((10, 6, 9, 11), (14, 2, 5, 7), (13, 15, 8, 3), (1, 4, 12, 0)):
        done = []
        for k in group:
            p = lax.rem(y + k, NY)
            cut = cuts(p)
            edge = zero_tile
            windows = []
            for i in range(B + 2):
                window, edge = pack(natt.at[i], cut, i, edge)
                windows.append(window)
            done.append((k, p, windows + [edge]))
        for k, p, windows in done:
            for i, window in enumerate(windows):
                tst[p, i] = window
            for copy in t_own if k == 0 else t_moves[k - 1]:
                copy.start()

    for copy in u_own:
        copy.wait()
    for copies in u_moves:
        for copy in copies:
            copy.wait_recv()
    inner = pl.ds(8, 128)

    u_planes = plane_copies(u, lambda i: (slice(None), i, inner), ps, pr)
    for copy in u_planes:
        copy.start()

    length = tally[y]
    wide_lane = lax.broadcasted_iota(jnp.int32, (128, 128), 1)
    edges = ue[inner]

    def disp(a, i):
        own = u[a, i + 1, inner]
        plus, minus = beside(own, edges, a * 8 + i, length, wide_lane)
        total = (
            u[a, i + 2, inner] + u[a, i, inner] + u[a, i + 1, pl.ds(9, 128)] + u[a, i + 1, pl.ds(7, 128)]
            + plus + minus
        )
        return mu[i] * (6.0 * own - total)

    for a in range(3):
        def disp_rows(step, _, a=a):
            first = 1 + 2 * step
            done = [disp(a, first), disp(a, first + 1)]
            for i, value in enumerate(done):
                r_out[a, first + i] = value
            return 0
        lax.fori_loop(0, B // 2 - 1, disp_rows, 0)

    for copy in u_planes:
        copy.wait_recv()
    for a in range(3):
        u[a, 0, inner] = u[a, 0, inner] * inside_low_g
        u[a, B + 1, inner] = u[a, B + 1, inner] * inside_high_g
        done = [disp(a, 0), disp(a, B - 1)]
        r_out[a, 0] = done[0]
        r_out[a, B - 1] = done[1]

    valid = wide_lane < length

    for copy in t_own:
        copy.wait()
    for copies in t_moves:
        for copy in copies:
            copy.wait_recv()

    for i in range(B + 2):
        t[i, inner] = beta[i] * t[i, inner]

    def stress_rows(step, _):
        done = []
        for i in (2 * step, 2 * step + 1):
            plus, minus = beside(t[i + 1, inner], beta[i + 1] * t[B + 2, inner], i + 1, length, wide_lane)
            along_i = t[i + 2, inner] - t[i, inner]
            along_j = t[i + 1, pl.ds(9, 128)] - t[i + 1, pl.ds(7, 128)]
            for a, v in enumerate((along_i, along_j, plus - minus)):
                done.append((a, i, jnp.where(valid, r_out[a, i] + 0.5 * v, 0.0)))
        for a, i, value in done:
            r_out[a, i] = value
        return 0
    lax.fori_loop(0, B // 2, stress_rows, 0)

    for copy in k_moves + k_relayed + c_moves + c_relayed + v0_moves + v0_relayed + v1_moves + v1_relayed:
        copy.wait_send()
    for copy in ar1_moves + ar2_moves + u_planes:
        copy.wait_send()
    for copies in u_moves + t_moves:
        for copy in copies:
            copy.wait_send()


def beside(own, edges, at, length, lane):
    nxt = pltpu.roll(edges, (length - 1 - 32 - at + 256) & 127, 1)
    prev = pltpu.roll(edges, (128 - at) & 127, 1)
    plus = jnp.where(lane == length - 1, nxt, pltpu.roll(own, 127, 1))
    minus = jnp.where(lane == 0, prev, pltpu.roll(own, 1, 1))
    return plus, minus


def local(
    starting_warmth_level,
    diffusive_coefficient_map,
    specific_warmth_store,
    energy_source_flux,
    deformation_vector,
    substance_label_columns,
    substance_moduli_table,
    subdomain_point_tally,
):
    hbm = pl.BlockSpec(memory_space=pl.ANY)
    vmem = pl.BlockSpec(memory_space=pltpu.VMEM)
    smem = pl.BlockSpec(memory_space=pltpu.SMEM)
    grid = pltpu.VMEM((N, N, 8, 128), F32)
    dma = pltpu.SemaphoreType.DMA
    return pl.pallas_call(
        kernel,
        out_shape=(
            pltpu.VMEM((B, B, KT * 128), F32),
            pltpu.VMEM((3, B, NY * 8, ZMAX), F32),
        ),
        in_specs=[hbm] * 5 + [vmem, smem, smem],
        out_specs=(vmem, vmem),
        scratch_shapes=[
            pltpu.VMEM((4, B, KT * 8, 128), F32),
            pltpu.VMEM((3, B, KT + 2, 8, 128), F32),
            grid, grid, grid, grid, grid, grid,
            pltpu.VMEM((LEVELS, N, N, 8, 128), F32),
            grid, grid, grid, grid, grid,
            pltpu.VMEM((NY, 3, B, 8, 128), F32),
            pltpu.VMEM((NY, 8, 128), F32),
            pltpu.VMEM((3, B + 2, 8 + 128 + 8, 128), F32),
            pltpu.VMEM((8 + 128 + 8, 128), F32),
            pltpu.VMEM((NY, B + 3, 8, 128), F32),
            pltpu.VMEM((B + 3, 8 + 128 + 8, 128), F32),
            pltpu.VMEM((B + 2, KT + 2, 8, 128), F32),
            pltpu.VMEM((B + 2, B * 8, 128), F32),
            pltpu.VMEM((B, 128, 128), F32),
            pltpu.VMEM((B + 2, 128, 128), F32),
            pltpu.VMEM((NY, 8, 128), F32),
            pltpu.VMEM((NG, 8, 128), F32),
            pltpu.VMEM((2, 8, 128), F32),
            pltpu.VMEM((1 + 2 * LEVELS, 8, 128), F32),
            pltpu.SMEM((NY,), jnp.int32),
            dma((4, KT)), dma((KT,)),
            dma((5, 12)), dma((5, 12)),
            dma((NY - 1,)), dma((NY - 1,)), dma((NG - 1,)), dma((NG - 1,)),
            dma((NY,)), dma((NY,)), dma((NY,)), dma((NY,)),
            dma((NY,)), dma((NY,)),
            dma((2,)), dma((2,)), dma((2,)), dma((2,)),
        ],
        compiler_params=pltpu.CompilerParams(
            collective_id=0, has_side_effects=True, vmem_limit_bytes=60 * 2**20
        ),
    )(
        starting_warmth_level,
        diffusive_coefficient_map,
        specific_warmth_store,
        energy_source_flux,
        deformation_vector,
        substance_label_columns,
        substance_moduli_table,
        subdomain_point_tally,
    )


def solution(mesh):
    placed = (
        P("gx", "yz", None),
        P("gx", "yz", None),
        P("gx", "yz", None),
        P("gx", "yz", None),
        P(None, "gx", "yz", None),
        P("gx", None),
        P(),
        P(),
    )
    return jax.shard_map(
        local,
        mesh=mesh,
        in_specs=placed,
        out_specs=(P("gx", "yz", None), P(None, "gx", None, "yz")),
        check_vma=False,
    )
```

```python
import functools

import jax
import jax.numpy as jnp
from jax import lax
from jax.experimental import pallas as pl
from jax.experimental.pallas import tpu as pltpu
from jax.sharding import PartitionSpec as P

NCHEB = 6
ZMAX = 128
NG, NY = 8, 16
B = 8
H = 6
N = B + 2 * H
LO, HI = H, H + B
KT = 8
LEVELS = NCHEB - 1
MESH = pl.DeviceIdType.MESH
F32 = jnp.float32


def corner_rects(width):
    if width == 6:
        return [(1, 2, 5), (3, 5, 3)]
    if width == 5:
        return [(1, 2, 4), (3, 4, 2)]
    return []


def kernel(
    x0_hbm, k_hbm, c_hbm, f_hbm, u_hbm, lab, table, tally,
    t_out, r_out,
    nat, natu, kb, cb, xb, fb, v0, v1, e, rb, fx, fy, fz, db,
    ust, uest, u, ue, tst, t, natt, ytr,
    mu, beta, ar1, ar2, arst, coefs, starts,
    lsem, lusem, hs, hr, a1s, a1r, a2s, a2r, us, ur, ues, uer, ts, tr, ps, pr, bs, br,
):
    g, y = lax.axis_index("gx"), lax.axis_index("yz")
    gp, gm = lax.rem(g + 1, NG), lax.rem(g + NG - 1, NG)
    yp, ym = lax.rem(y + 1, NY), lax.rem(y + NY - 1, NY)
    def shifted(k):
        return lax.rem(y // 4 + k // 4, 4) * 4 + lax.rem(y + k % 4, 4)

    along_y = [(g, shifted(k)) for k in range(1, NY)]
    along_g = [(lax.rem(g + k, NG), y) for k in range(1, NG)]
    core = lax.rem(g, 2)
    sibling = (g + 1 - 2 * core, y)
    across = lax.rem(g + 2 * core - 1 + NG, NG)
    diagonal = [(across, yp), (across, ym)]

    fields = [k_hbm, x0_hbm, c_hbm, f_hbm]
    own_in = [
        [
            pltpu.make_async_copy(
                field.at[:, :, pl.ds(kt * 128, 128)], nat.at[n, :, pl.ds(kt * 8, 8)], lsem.at[n, kt]
            )
            for kt in range(KT)
        ]
        for n, field in enumerate(fields)
    ]
    u_in = [
        pltpu.make_async_copy(
            u_hbm.at[:, :, :, pl.ds(kt * 128, 128)], natu.at[:, :, kt + 1], lusem.at[kt]
        )
        for kt in range(KT)
    ]
    for copies in own_in:
        for copy in copies:
            copy.start()
    for copy in u_in:
        copy.start()

    barrier = pltpu.get_barrier_semaphore()
    for peer in along_y + along_g + diagonal:
        pl.semaphore_signal(barrier, inc=1, device_id=peer, device_id_type=MESH)

    zero_tile = jnp.zeros((8, 128), F32)
    for a in range(3):
        def zero_u(i, _, a=a):
            u[a, i, pl.ds(0, 8)] = zero_tile
            u[a, i, pl.ds(8 + 128, 8)] = zero_tile
            return 0
        lax.fori_loop(0, B + 2, zero_u, 0)

        def zero_natu(i, _, a=a):
            natu[a, i, 0] = zero_tile
            natu[a, i, KT + 1] = zero_tile
            return 0
        lax.fori_loop(0, B, zero_natu, 0)

    def zero_t(i, _):
        t[i, pl.ds(0, 8)] = zero_tile
        t[i, pl.ds(8 + 128, 8)] = zero_tile
        return 0
    lax.fori_loop(0, B + 2, zero_t, 0)

    def zero_natt(i, _):
        natt[i, 0] = zero_tile
        natt[i, KT + 1] = zero_tile
        return 0
    lax.fori_loop(0, B + 2, zero_natt, 0)

    def to_lines(n, dst):
        def row(i, _):
            for j in range(B):
                dst[LO + i, LO + j] = nat[n, i, pl.ds(j, 8, stride=8), :]
            return 0
        lax.fori_loop(0, B, row, 0)

    for n, dst in ((0, kb), (1, xb), (2, cb), (3, fb)):
        for copy in own_in[n]:
            copy.wait()
        to_lines(n, dst)

    pl.semaphore_wait(barrier, len(along_y) + len(along_g) + len(diagonal))

    def halo(buf, width, slot, width_j=None):
        def sides(w):
            return pl.ds(LO - w, w), pl.ds(HI, w), pl.ds(LO, w), pl.ds(HI - w, w)

        own = pl.ds(LO, B)
        low_i, high_i, first_i, last_i = sides(width)
        low_j, high_j, first_j, last_j = sides(width_j or width)
        moves = [
            (buf.at[own, last_j], buf.at[own, low_j], (g, yp)),
            (buf.at[own, first_j], buf.at[own, high_j], (g, ym)),
            (buf.at[last_i, own], buf.at[low_i, own], (gp, y)),
            (buf.at[first_i, own], buf.at[high_i, own], (gm, y)),
        ]
        relayed = []
        for a0, a1, b1 in corner_rects(width):
            rows = a1 - a0 + 1
            in_low, out_low, in_high, out_high = LO + a0 - 1, LO - a1, HI - a1, HI - 1 + a0
            to_across, at_across = in_low + core * (in_high - in_low), out_high + core * (out_low - out_high)
            to_sibling, at_sibling = in_high + core * (in_low - in_high), out_low + core * (out_high - out_low)
            low, high, first, last = (pl.ds(LO - b1, b1), pl.ds(HI, b1), pl.ds(LO, b1), pl.ds(HI - b1, b1))
            src, dst = pl.ds(to_across, rows), pl.ds(at_across, rows)
            moves += [
                (buf.at[src, last], buf.at[dst, low], diagonal[0]),
                (buf.at[src, first], buf.at[dst, high], diagonal[1]),
            ]
            src, dst = pl.ds(to_sibling, rows), pl.ds(at_sibling, rows)
            relayed += [(buf.at[src, low], buf.at[dst, low], sibling), (buf.at[src, high], buf.at[dst, high], sibling)]
        copies = [
            pltpu.make_async_remote_copy(
                src_ref=src, dst_ref=dst, send_sem=hs.at[slot, m], recv_sem=hr.at[slot, m],
                device_id=peer, device_id_type=MESH,
            )
            for m, (src, dst, peer) in enumerate(moves + relayed)
        ]
        return copies[:len(moves)], copies[len(moves):]

    def relay_start(moves, relayed):
        for copy in moves[:2]:
            copy.wait_recv()
        for copy in relayed:
            copy.start()

    def relay(moves, relayed, ks):
        relay_start(moves, relayed)
        send_u(ks)
        for copy in moves[2:] + relayed:
            copy.wait_recv()

    def plane_copies(buf, at, send, recv):
        return [
            pltpu.make_async_remote_copy(
                src_ref=buf.at[at(B)], dst_ref=buf.at[at(0)],
                send_sem=send.at[0], recv_sem=recv.at[0], device_id=(gp, y), device_id_type=MESH,
            ),
            pltpu.make_async_remote_copy(
                src_ref=buf.at[at(1)], dst_ref=buf.at[at(B + 1)],
                send_sem=send.at[1], recv_sem=recv.at[1], device_id=(gm, y), device_id_type=MESH,
            ),
        ]

    x0_moves, _ = halo(xb, 1, 0)
    k_moves, k_relayed = halo(kb, 6, 1)
    c_moves, c_relayed = halo(cb, 5, 2)
    for copy in x0_moves + k_moves + c_moves:
        copy.start()

    total = jnp.int32(0)
    for p in range(NY):
        starts[p] = total
        total = total + tally[p]

    eye = lax.broadcasted_iota(jnp.int32, (128, 128), 0) == lax.broadcasted_iota(jnp.int32, (128, 128), 1)

    def column_row(i, _):
        row = jnp.broadcast_to(lab[pl.ds(i, 1), :].astype(F32), (128, 128))
        column = jnp.sum(jnp.where(eye, row, 0.0), axis=1, keepdims=True)
        label = jnp.broadcast_to(column, (128, 128))
        for dst, r, at in ((mu, 0, i), (beta, 1, i + 1)):
            dst[at] = jnp.where(label == 0.0, table[r, 0], 0.0) + jnp.where(label == 1.0, table[r, 1], 0.0)
        return 0
    lax.fori_loop(0, B, column_row, 0)
    beta_planes = plane_copies(beta, lambda i: (i,), bs, br)
    for copy in beta_planes:
        copy.start()

    lane = lax.broadcasted_iota(jnp.int32, (8, 128), 1)

    def cuts(p):
        start = starts[p]
        before, after = start + 127, start + tally[p] + 128
        return (start >> 7) + 1, start & 127, before >> 7, before & 127, after >> 7, after & 127

    def pack(line, cut, lane_of, edge):
        tile, off, tile_before, lane_before, tile_after, lane_after = cut
        window = jnp.where(lane >= off, line[tile], line[tile + 1])
        prev = pltpu.roll(line[tile_before], (lane_of - lane_before + 256) & 127, 1)
        nxt = pltpu.roll(line[tile_after], (32 + lane_of - lane_after + 256) & 127, 1)
        edge = jnp.where(lane == lane_of, prev, jnp.where(lane == lane_of + 32, nxt, edge))
        return pltpu.roll(window, (128 - off) & 127, 1), edge

    for copy in u_in:
        copy.wait()

    def pack_u(p, _):
        cut = cuts(p)
        edge = zero_tile
        for a in range(3):
            for i in range(B):
                ust[p, a, i], edge = pack(natu.at[a, i], cut, a * 8 + i, edge)
        uest[p] = edge
        return 0
    lax.fori_loop(0, NY, pack_u, 0)

    rows_of_me = pl.ds(pl.multiple_of(8 + 8 * y, 8), 8)

    def u_copies(k):
        p = shifted(k)
        peer = (g, p)
        return [
            pltpu.make_async_remote_copy(
                src_ref=ust.at[p], dst_ref=u.at[:, pl.ds(1, B), rows_of_me],
                send_sem=us.at[k], recv_sem=ur.at[k], device_id=peer, device_id_type=MESH,
            ),
            pltpu.make_async_remote_copy(
                src_ref=uest.at[p], dst_ref=ue.at[rows_of_me],
                send_sem=ues.at[k], recv_sem=uer.at[k], device_id=peer, device_id_type=MESH,
            ),
        ]

    u_moves = [u_copies(k) for k in range(1, NY)]
    u_own = [
        pltpu.make_async_copy(ust.at[y], u.at[:, pl.ds(1, B), rows_of_me], us.at[0]),
        pltpu.make_async_copy(uest.at[y], ue.at[rows_of_me], ues.at[0]),
    ]
    def send_u(ks):
        for k in ks:
            for copy in u_moves[k - 1]:
                copy.start()

    send_u((4, 12, 8))
    for copy in u_own:
        copy.start()

    def iota(n, axis):
        return lax.broadcasted_iota(jnp.int32, (n, 8, 128), axis)

    def up(v):
        by_lane = pltpu.roll(v, 127, 2)
        return jnp.where(iota(v.shape[0], 2) == 127, pltpu.roll(by_lane, 7, 1), by_lane)

    def down(v):
        by_lane = pltpu.roll(v, 1, 2)
        return jnp.where(iota(v.shape[0], 2) == 0, pltpu.roll(by_lane, 1, 1), by_lane)

    def harmonic(first, second):
        return 2.0 * first * second / (first + second)

    inside_low_g = jnp.where(g > 0, 1.0, 0.0)
    inside_high_g = jnp.where(g < NG - 1, 1.0, 0.0)
    inside_low_y = jnp.where(y > 0, 1.0, 0.0)
    inside_high_y = jnp.where(y < NY - 1, 1.0, 0.0)

    def faces(q):
        lo, n = LO - q, B + 2 * q

        whole = pl.ds(lo, n)
        fx[lo - 1, whole] = harmonic(kb[lo - 1, whole], kb[lo, whole])

        def fx_rows(step, _):
            i = lo + 2 * step
            low, high = harmonic(kb[i, whole], kb[i + 1, whole]), harmonic(kb[i + 1, whole], kb[i + 2, whole])
            fx[i, whole] = low
            fx[i + 1, whole] = high
            return 0
        lax.fori_loop(0, n // 2, fx_rows, 0)

        fx[LO - 1, pl.ds(lo, n)] = fx[LO - 1, pl.ds(lo, n)] * inside_low_g
        fx[HI - 1, pl.ds(lo, n)] = fx[HI - 1, pl.ds(lo, n)] * inside_high_g

        last = (iota(n, 1) == 7) & (iota(n, 2) == 127)

        def rows(step, _):
            first = lo + 2 * step
            done = []
            for i in (first, first + 1):
                own = kb[i, whole]
                low = harmonic(kb[i, lo - 1], kb[i, lo])
                along_j = harmonic(own, kb[i, pl.ds(lo + 1, n)])
                along_k = jnp.where(last, 0.0, harmonic(own, up(own)))
                done.append((low, along_j, along_k, cb[i, whole] + fx[i, whole] + fx[i - 1, whole] + along_k + down(along_k)))
            for i, (low, along_j, along_k, others) in enumerate(done):
                i = first + i
                fy[i, lo - 1] = low
                fy[i, whole] = along_j
                fz[i, whole] = along_k
                db[i, whole] = others
            return 0
        lax.fori_loop(0, n // 2, rows, 0)

        span = pl.ds(lo, n)
        fy[span, LO - 1] = fy[span, LO - 1] * inside_low_y
        fy[span, HI - 1] = fy[span, HI - 1] * inside_high_y

        def diagonal_row(i, _):
            db[i, whole] = db[i, whole] + fy[i, whole] + fy[i, pl.ds(lo - 1, n)]
            return 0
        lax.fori_loop(lo, lo + n, diagonal_row, 0)

    def applied(v, i, j0, c):
        at = pl.ds(j0, c)
        own, z = v[i, at], fz[i, at]
        return (
            db[i, at] * own
            - fx[i, at] * v[i + 1, at]
            - fx[i - 1, at] * v[i - 1, at]
            - fy[i, at] * v[i, pl.ds(j0 + 1, c)]
            - fy[i, pl.ds(j0 - 1, c)] * v[i, pl.ds(j0 - 1, c)]
            - z * up(own)
            - down(z * own)
        )

    def first_residual(x, dst):
        at = pl.ds(LO, B)
        done = [fb[i, at] + (cb[i, at] * x[i, at] - applied(x, i, LO, B)) for i in range(LO, HI)]
        for i, value in enumerate(done):
            dst[LO + i, at] = value

    for copy in x0_moves + k_moves[:4]:
        copy.wait_recv()
    for copy in k_relayed:
        copy.start()
    faces(0)

    def bound_row(i, carry):
        most, least = carry
        at = pl.ds(LO, B)
        c = cb[i, at]
        return (
            jnp.maximum(most, jnp.max(2.0 * db[i, at] - c, axis=0)),
            jnp.maximum(least, jnp.max(-c, axis=0)),
        )
    neg = jnp.full((8, 128), -3.0e38, F32)
    most, least = lax.fori_loop(LO, HI, bound_row, (neg, neg))
    sub = lax.broadcasted_iota(jnp.int32, (8, 128), 0)

    def over_rows(v):
        return jnp.broadcast_to(jnp.max(v, axis=0, keepdims=True), (8, 128))

    arst[0] = jnp.where(sub < 4, over_rows(most), over_rows(least))
    ar1[y] = arst[0]
    ar1_moves = [
        pltpu.make_async_remote_copy(
            src_ref=arst.at[0], dst_ref=ar1.at[y], send_sem=a1s.at[k], recv_sem=a1r.at[k],
            device_id=peer, device_id_type=MESH,
        )
        for k, peer in enumerate(along_y)
    ]
    for copy in ar1_moves:
        copy.start()

    first_residual(xb, v0)
    v0_moves, v0_relayed = halo(v0, 6, 3)
    for copy in v0_moves:
        copy.start()

    send_u((1, 3, 5, 15))
    relay_start(c_moves, c_relayed)
    for copy in ar1_moves:
        copy.wait_recv()
    arst[1] = jnp.max(ar1[...], axis=0)
    ar2[g] = arst[1]
    ar2_moves = [
        pltpu.make_async_remote_copy(
            src_ref=arst.at[1], dst_ref=ar2.at[g], send_sem=a2s.at[k], recv_sem=a2r.at[k],
            device_id=peer, device_id_type=MESH,
        )
        for k, peer in enumerate(along_g)
    ]
    for copy in ar2_moves:
        copy.start()
    for copy in c_moves[2:] + c_relayed + k_moves[4:] + k_relayed:
        copy.wait_recv()
    faces(5)

    for copy in ar2_moves:
        copy.wait_recv()
    send_u((7, 13, 2, 10))
    for copy in beta_planes:
        copy.wait()
    beta[0] = beta[0] * inside_low_g
    beta[B + 1] = beta[B + 1] * inside_high_g

    bounds = jnp.max(jnp.max(ar2[...], axis=0), axis=1, keepdims=True)
    high = jnp.broadcast_to(bounds[0:1], (8, 128))
    low = -jnp.broadcast_to(bounds[4:5], (8, 128))
    theta = (high + low) / 2.0
    delta = (high - low) / 2.0
    sigma = theta / delta
    rho = 1.0 / sigma
    coefs[0] = 1.0 / theta
    for turn in range(LEVELS):
        rho_new = 1.0 / (2.0 * sigma - rho)
        coefs[1 + 2 * turn] = rho_new * rho
        coefs[2 + 2 * turn] = 2.0 * rho_new / delta * theta
        rho = rho_new

    def level(src, turn, qi, qj):
        lo, n = LO - qi, B + 2 * qi
        rows = max(d for d in range(1, 10) if n % d == 0)
        j0, c = LO - qj, B + 2 * qj
        at = pl.ds(j0, c)
        inv, alpha, bet = coefs[0], coefs[1 + 2 * turn], coefs[2 + 2 * turn]
        before = src if turn == 0 else rb

        def some_rows(step, _):
            first = lo + step * rows
            done = []
            for i in range(rows):
                resid = before[first + i, at] - inv[None] * applied(src, first + i, j0, c)
                done.append((resid, alpha[None] * src[first + i, at] + bet[None] * resid))
            for i, (resid, value) in enumerate(done):
                rb[first + i, at] = resid
                e[turn, first + i, at] = value
            return 0
        lax.fori_loop(0, n // rows, some_rows, 0)

    def heat_step(start, qi, qj):
        src = start
        for turn in range(LEVELS):
            level(src, turn, qi - 1 - turn, qj - 1 - turn)
            src = e.at[turn]

    def summed(start, i, at):
        total = start[i, at]
        for turn in range(LEVELS):
            total = total + e[turn, i, at]
        return xb[i, at] + coefs[0][None] * total

    relay(v0_moves, v0_relayed, (9, 11))
    heat_step(v0, 6, 6)

    for copy in x0_moves:
        copy.wait_send()

    def next_x(i, _):
        at = pl.ds(LO - 1, B + 2)
        xb[i, at] = summed(v0, i, at)
        return 0
    lax.fori_loop(LO - 1, HI + 1, next_x, 0)

    first_residual(xb, v1)
    v1_moves, v1_relayed = halo(v1, 6, 4, 5)
    for copy in v1_moves:
        copy.start()
    relay(v1_moves, v1_relayed, (6, 14))
    heat_step(v1, 6, 5)

    def last_x(i, _):
        final = summed(v1, LO - 1 + i, pl.ds(LO, B))
        for j in range(B):
            ytr[i, pl.ds(j * 8, 8)] = final[j]
        return 0
    lax.fori_loop(0, B + 2, last_x, 0)

    def to_natural(i, _):
        for kt in range(KT):
            natt[i, kt + 1] = ytr[i, pl.ds(kt, 8, stride=8), :]
        return 0
    lax.fori_loop(0, B + 2, to_natural, 0)

    for kt in range(KT):
        t_out[:, :, pl.ds(kt * 128, 128)] = natt[pl.ds(1, B), kt + 1]

    def t_copies(k):
        p = shifted(k)
        peer = (g, p)
        return [
            pltpu.make_async_remote_copy(
                src_ref=tst.at[p], dst_ref=t.at[:, rows_of_me],
                send_sem=ts.at[k], recv_sem=tr.at[k], device_id=peer, device_id_type=MESH,
            )
        ]

    t_moves = [t_copies(k) for k in range(1, NY)]
    t_own = [
        pltpu.make_async_copy(tst.at[y], t.at[:, rows_of_me], ts.at[0]),
    ]
    for group in ((10, 6, 9, 11), (14, 2, 5, 7), (13, 15, 8, 3), (1, 4, 12, 0)):
        done = []
        for k in group:
            p = shifted(k)
            cut = cuts(p)
            edge = zero_tile
            windows = []
            for i in range(B + 2):
                window, edge = pack(natt.at[i], cut, i, edge)
                windows.append(window)
            done.append((k, p, windows + [edge]))
        for k, p, windows in done:
            for i, window in enumerate(windows):
                tst[p, i] = window
            for copy in t_own if k == 0 else t_moves[k - 1]:
                copy.start()

    for copy in u_own:
        copy.wait()
    for copies in u_moves:
        for copy in copies:
            copy.wait_recv()
    inner = pl.ds(8, 128)

    u_planes = plane_copies(u, lambda i: (slice(None), i, inner), ps, pr)
    for copy in u_planes:
        copy.start()

    length = tally[y]
    wide_lane = lax.broadcasted_iota(jnp.int32, (128, 128), 1)
    edges = ue[inner]

    def disp(a, i):
        own = u[a, i + 1, inner]
        plus, minus = beside(own, edges, a * 8 + i, length, wide_lane)
        total = (
            u[a, i + 2, inner] + u[a, i, inner] + u[a, i + 1, pl.ds(9, 128)] + u[a, i + 1, pl.ds(7, 128)]
            + plus + minus
        )
        return mu[i] * (6.0 * own - total)

    for a in range(3):
        def disp_rows(step, _, a=a):
            first = 1 + 2 * step
            done = [disp(a, first), disp(a, first + 1)]
            for i, value in enumerate(done):
                r_out[a, first + i] = value
            return 0
        lax.fori_loop(0, B // 2 - 1, disp_rows, 0)

    for copy in u_planes:
        copy.wait_recv()
    for a in range(3):
        u[a, 0, inner] = u[a, 0, inner] * inside_low_g
        u[a, B + 1, inner] = u[a, B + 1, inner] * inside_high_g
        done = [disp(a, 0), disp(a, B - 1)]
        r_out[a, 0] = done[0]
        r_out[a, B - 1] = done[1]

    valid = wide_lane < length

    for copy in t_own:
        copy.wait()
    for copies in t_moves:
        for copy in copies:
            copy.wait_recv()

    for i in range(B + 2):
        t[i, inner] = beta[i] * t[i, inner]

    def stress_rows(step, _):
        done = []
        for i in (2 * step, 2 * step + 1):
            plus, minus = beside(t[i + 1, inner], beta[i + 1] * t[B + 2, inner], i + 1, length, wide_lane)
            along_i = t[i + 2, inner] - t[i, inner]
            along_j = t[i + 1, pl.ds(9, 128)] - t[i + 1, pl.ds(7, 128)]
            for a, v in enumerate((along_i, along_j, plus - minus)):
                done.append((a, i, jnp.where(valid, r_out[a, i] + 0.5 * v, 0.0)))
        for a, i, value in done:
            r_out[a, i] = value
        return 0
    lax.fori_loop(0, B // 2, stress_rows, 0)

    for copy in k_moves + k_relayed + c_moves + c_relayed + v0_moves + v0_relayed + v1_moves + v1_relayed:
        copy.wait_send()
    for copy in ar1_moves + ar2_moves + u_planes:
        copy.wait_send()
    for copies in u_moves + t_moves:
        for copy in copies:
            copy.wait_send()


def beside(own, edges, at, length, lane):
    nxt = pltpu.roll(edges, (length - 1 - 32 - at + 256) & 127, 1)
    prev = pltpu.roll(edges, (128 - at) & 127, 1)
    plus = jnp.where(lane == length - 1, nxt, pltpu.roll(own, 127, 1))
    minus = jnp.where(lane == 0, prev, pltpu.roll(own, 1, 1))
    return plus, minus


def local(
    starting_warmth_level,
    diffusive_coefficient_map,
    specific_warmth_store,
    energy_source_flux,
    deformation_vector,
    substance_label_columns,
    substance_moduli_table,
    subdomain_point_tally,
):
    hbm = pl.BlockSpec(memory_space=pl.ANY)
    vmem = pl.BlockSpec(memory_space=pltpu.VMEM)
    smem = pl.BlockSpec(memory_space=pltpu.SMEM)
    grid = pltpu.VMEM((N, N, 8, 128), F32)
    dma = pltpu.SemaphoreType.DMA
    return pl.pallas_call(
        kernel,
        out_shape=(
            pltpu.VMEM((B, B, KT * 128), F32),
            pltpu.VMEM((3, B, NY * 8, ZMAX), F32),
        ),
        in_specs=[hbm] * 5 + [vmem, smem, smem],
        out_specs=(vmem, vmem),
        scratch_shapes=[
            pltpu.VMEM((4, B, KT * 8, 128), F32),
            pltpu.VMEM((3, B, KT + 2, 8, 128), F32),
            grid, grid, grid, grid, grid, grid,
            pltpu.VMEM((LEVELS, N, N, 8, 128), F32),
            grid, grid, grid, grid, grid,
            pltpu.VMEM((NY, 3, B, 8, 128), F32),
            pltpu.VMEM((NY, 8, 128), F32),
            pltpu.VMEM((3, B + 2, 8 + 128 + 8, 128), F32),
            pltpu.VMEM((8 + 128 + 8, 128), F32),
            pltpu.VMEM((NY, B + 3, 8, 128), F32),
            pltpu.VMEM((B + 3, 8 + 128 + 8, 128), F32),
            pltpu.VMEM((B + 2, KT + 2, 8, 128), F32),
            pltpu.VMEM((B + 2, B * 8, 128), F32),
            pltpu.VMEM((B, 128, 128), F32),
            pltpu.VMEM((B + 2, 128, 128), F32),
            pltpu.VMEM((NY, 8, 128), F32),
            pltpu.VMEM((NG, 8, 128), F32),
            pltpu.VMEM((2, 8, 128), F32),
            pltpu.VMEM((1 + 2 * LEVELS, 8, 128), F32),
            pltpu.SMEM((NY,), jnp.int32),
            dma((4, KT)), dma((KT,)),
            dma((5, 12)), dma((5, 12)),
            dma((NY - 1,)), dma((NY - 1,)), dma((NG - 1,)), dma((NG - 1,)),
            dma((NY,)), dma((NY,)), dma((NY,)), dma((NY,)),
            dma((NY,)), dma((NY,)),
            dma((2,)), dma((2,)), dma((2,)), dma((2,)),
        ],
        compiler_params=pltpu.CompilerParams(
            collective_id=0, has_side_effects=True, vmem_limit_bytes=60 * 2**20
        ),
    )(
        starting_warmth_level,
        diffusive_coefficient_map,
        specific_warmth_store,
        energy_source_flux,
        deformation_vector,
        substance_label_columns,
        substance_moduli_table,
        subdomain_point_tally,
    )


def solution(mesh):
    placed = (
        P("gx", "yz", None),
        P("gx", "yz", None),
        P("gx", "yz", None),
        P("gx", "yz", None),
        P(None, "gx", "yz", None),
        P("gx", None),
        P(),
        P(),
    )
    return jax.shard_map(
        local,
        mesh=mesh,
        in_specs=placed,
        out_specs=(P("gx", "yz", None), P(None, "gx", None, "yz")),
        check_vma=False,
    )
```

```python
import functools

import jax
import jax.numpy as jnp
from jax import lax
from jax.experimental import pallas as pl
from jax.experimental.pallas import tpu as pltpu
from jax.sharding import PartitionSpec as P

NCHEB = 6
ZMAX = 128
NG, NY = 8, 16
B = 8
H = 6
N = B + 2 * H
LO, HI = H, H + B
KT = 8
LEVELS = NCHEB - 1
MESH = pl.DeviceIdType.MESH
F32 = jnp.float32


def corner_rects(width):
    if width == 6:
        return [(1, 2, 5), (3, 5, 3)]
    if width == 5:
        return [(1, 2, 4), (3, 4, 2)]
    return []


def kernel(
    x0_hbm, k_hbm, c_hbm, f_hbm, u_hbm, lab, table, tally,
    t_out, r_out,
    nat, natu, kb, cb, xb, fb, v0, v1, e, rb, fx, fy, fz, db,
    ust, uest, u, ue, tst, t, natt, ytr,
    mu, beta, ar1, ar2, arst, coefs, starts,
    lsem, lusem, hs, hr, a1s, a1r, a2s, a2r, us, ur, ues, uer, ts, tr, ps, pr, bs, br,
):
    g, y = lax.axis_index("gx"), lax.axis_index("yz")
    gp, gm = lax.rem(g + 1, NG), lax.rem(g + NG - 1, NG)
    yp, ym = lax.rem(y + 1, NY), lax.rem(y + NY - 1, NY)
    def shifted(k):
        return lax.rem(y // 4 + k // 4, 4) * 4 + lax.rem(y + k % 4, 4)

    along_y = [(g, shifted(k)) for k in range(1, NY)]
    along_g = [(lax.rem(g + k, NG), y) for k in range(1, NG)]
    core = lax.rem(g, 2)
    sibling = (g + 1 - 2 * core, y)
    across = lax.rem(g + 2 * core - 1 + NG, NG)
    diagonal = [(across, yp), (across, ym)]

    fields = [k_hbm, x0_hbm, c_hbm, f_hbm]
    own_in = [
        [
            pltpu.make_async_copy(
                field.at[:, :, pl.ds(kt * 128, 128)], nat.at[n, :, pl.ds(kt * 8, 8)], lsem.at[n, kt]
            )
            for kt in range(KT)
        ]
        for n, field in enumerate(fields)
    ]
    u_in = [
        pltpu.make_async_copy(
            u_hbm.at[:, :, :, pl.ds(kt * 128, 128)], natu.at[:, :, kt + 1], lusem.at[kt]
        )
        for kt in range(KT)
    ]
    for copies in own_in:
        for copy in copies:
            copy.start()
    for copy in u_in:
        copy.start()

    barrier = pltpu.get_barrier_semaphore()
    for peer in along_y + along_g + diagonal:
        pl.semaphore_signal(barrier, inc=1, device_id=peer, device_id_type=MESH)

    zero_tile = jnp.zeros((8, 128), F32)
    for a in range(3):
        def zero_u(i, _, a=a):
            u[a, i, pl.ds(0, 8)] = zero_tile
            u[a, i, pl.ds(8 + 128, 8)] = zero_tile
            return 0
        lax.fori_loop(0, B + 2, zero_u, 0)

        def zero_natu(i, _, a=a):
            natu[a, i, 0] = zero_tile
            natu[a, i, KT + 1] = zero_tile
            return 0
        lax.fori_loop(0, B, zero_natu, 0)

    def zero_t(i, _):
        t[i, pl.ds(0, 8)] = zero_tile
        t[i, pl.ds(8 + 128, 8)] = zero_tile
        return 0
    lax.fori_loop(0, B + 2, zero_t, 0)

    def zero_natt(i, _):
        natt[i, 0] = zero_tile
        natt[i, KT + 1] = zero_tile
        return 0
    lax.fori_loop(0, B + 2, zero_natt, 0)

    def to_lines(n, dst):
        def row(i, _):
            for j in range(B):
                dst[LO + i, LO + j] = nat[n, i, pl.ds(j, 8, stride=8), :]
            return 0
        lax.fori_loop(0, B, row, 0)

    for n, dst in ((0, kb), (1, xb), (2, cb), (3, fb)):
        for copy in own_in[n]:
            copy.wait()
        to_lines(n, dst)

    pl.semaphore_wait(barrier, len(along_y) + len(along_g) + len(diagonal))

    def halo(buf, width, slot, width_j=None):
        def sides(w):
            return pl.ds(LO - w, w), pl.ds(HI, w), pl.ds(LO, w), pl.ds(HI - w, w)

        own = pl.ds(LO, B)
        low_i, high_i, first_i, last_i = sides(width)
        low_j, high_j, first_j, last_j = sides(width_j or width)
        moves = [
            (buf.at[own, last_j], buf.at[own, low_j], (g, yp)),
            (buf.at[own, first_j], buf.at[own, high_j], (g, ym)),
            (buf.at[last_i, own], buf.at[low_i, own], (gp, y)),
            (buf.at[first_i, own], buf.at[high_i, own], (gm, y)),
        ]
        relayed = []
        for a0, a1, b1 in corner_rects(width):
            rows = a1 - a0 + 1
            in_low, out_low, in_high, out_high = LO + a0 - 1, LO - a1, HI - a1, HI - 1 + a0
            to_across, at_across = in_low + core * (in_high - in_low), out_high + core * (out_low - out_high)
            to_sibling, at_sibling = in_high + core * (in_low - in_high), out_low + core * (out_high - out_low)
            low, high, first, last = (pl.ds(LO - b1, b1), pl.ds(HI, b1), pl.ds(LO, b1), pl.ds(HI - b1, b1))
            src, dst = pl.ds(to_across, rows), pl.ds(at_across, rows)
            moves += [
                (buf.at[src, last], buf.at[dst, low], diagonal[0]),
                (buf.at[src, first], buf.at[dst, high], diagonal[1]),
            ]
            src, dst = pl.ds(to_sibling, rows), pl.ds(at_sibling, rows)
            relayed += [(buf.at[src, low], buf.at[dst, low], sibling), (buf.at[src, high], buf.at[dst, high], sibling)]
        copies = [
            pltpu.make_async_remote_copy(
                src_ref=src, dst_ref=dst, send_sem=hs.at[slot, m], recv_sem=hr.at[slot, m],
                device_id=peer, device_id_type=MESH,
            )
            for m, (src, dst, peer) in enumerate(moves + relayed)
        ]
        return copies[:len(moves)], copies[len(moves):]

    def relay_start(moves, relayed):
        for copy in moves[:2]:
            copy.wait_recv()
        for copy in relayed:
            copy.start()

    def relay(moves, relayed, ks):
        relay_start(moves, relayed)
        send_u(ks)
        for copy in moves[2:] + relayed:
            copy.wait_recv()

    def plane_copies(buf, at, send, recv):
        return [
            pltpu.make_async_remote_copy(
                src_ref=buf.at[at(B)], dst_ref=buf.at[at(0)],
                send_sem=send.at[0], recv_sem=recv.at[0], device_id=(gp, y), device_id_type=MESH,
            ),
            pltpu.make_async_remote_copy(
                src_ref=buf.at[at(1)], dst_ref=buf.at[at(B + 1)],
                send_sem=send.at[1], recv_sem=recv.at[1], device_id=(gm, y), device_id_type=MESH,
            ),
        ]

    x0_moves, _ = halo(xb, 1, 0)
    k_moves, k_relayed = halo(kb, 6, 1)
    c_moves, c_relayed = halo(cb, 5, 2)
    for copy in x0_moves + k_moves + c_moves:
        copy.start()

    total = jnp.int32(0)
    for p in range(NY):
        starts[p] = total
        total = total + tally[p]

    eye = lax.broadcasted_iota(jnp.int32, (128, 128), 0) == lax.broadcasted_iota(jnp.int32, (128, 128), 1)

    def column_row(i, _):
        row = jnp.broadcast_to(lab[pl.ds(i, 1), :].astype(F32), (128, 128))
        column = jnp.sum(jnp.where(eye, row, 0.0), axis=1, keepdims=True)
        label = jnp.broadcast_to(column, (128, 128))
        for dst, r, at in ((mu, 0, i), (beta, 1, i + 1)):
            dst[at] = jnp.where(label == 0.0, table[r, 0], 0.0) + jnp.where(label == 1.0, table[r, 1], 0.0)
        return 0
    lax.fori_loop(0, B, column_row, 0)
    beta_planes = plane_copies(beta, lambda i: (i,), bs, br)
    for copy in beta_planes:
        copy.start()

    lane = lax.broadcasted_iota(jnp.int32, (8, 128), 1)

    def cuts(p):
        start = starts[p]
        before, after = start + 127, start + tally[p] + 128
        return (start >> 7) + 1, start & 127, before >> 7, before & 127, after >> 7, after & 127

    def pack(line, cut, lane_of, edge):
        tile, off, tile_before, lane_before, tile_after, lane_after = cut
        window = jnp.where(lane >= off, line[tile], line[tile + 1])
        prev = pltpu.roll(line[tile_before], (lane_of - lane_before + 256) & 127, 1)
        nxt = pltpu.roll(line[tile_after], (32 + lane_of - lane_after + 256) & 127, 1)
        edge = jnp.where(lane == lane_of, prev, jnp.where(lane == lane_of + 32, nxt, edge))
        return pltpu.roll(window, (128 - off) & 127, 1), edge

    for copy in u_in:
        copy.wait()

    def pack_u(p, _):
        cut = cuts(p)
        edge = zero_tile
        for a in range(3):
            for i in range(B):
                ust[p, a, i], edge = pack(natu.at[a, i], cut, a * 8 + i, edge)
        uest[p] = edge
        return 0
    lax.fori_loop(0, NY, pack_u, 0)

    rows_of_me = pl.ds(pl.multiple_of(8 + 8 * y, 8), 8)

    def u_copies(k):
        p = shifted(k)
        peer = (g, p)
        return [
            pltpu.make_async_remote_copy(
                src_ref=ust.at[p], dst_ref=u.at[:, pl.ds(1, B), rows_of_me],
                send_sem=us.at[k], recv_sem=ur.at[k], device_id=peer, device_id_type=MESH,
            ),
            pltpu.make_async_remote_copy(
                src_ref=uest.at[p], dst_ref=ue.at[rows_of_me],
                send_sem=ues.at[k], recv_sem=uer.at[k], device_id=peer, device_id_type=MESH,
            ),
        ]

    u_moves = [u_copies(k) for k in range(1, NY)]
    u_own = [
        pltpu.make_async_copy(ust.at[y], u.at[:, pl.ds(1, B), rows_of_me], us.at[0]),
        pltpu.make_async_copy(uest.at[y], ue.at[rows_of_me], ues.at[0]),
    ]
    def send_u(ks):
        for k in ks:
            for copy in u_moves[k - 1]:
                copy.start()

    send_u((4, 12, 8))
    for copy in u_own:
        copy.start()

    def iota(n, axis):
        return lax.broadcasted_iota(jnp.int32, (n, 8, 128), axis)

    def up(v):
        by_lane = pltpu.roll(v, 127, 2)
        return jnp.where(iota(v.shape[0], 2) == 127, pltpu.roll(by_lane, 7, 1), by_lane)

    def down(v):
        by_lane = pltpu.roll(v, 1, 2)
        return jnp.where(iota(v.shape[0], 2) == 0, pltpu.roll(by_lane, 1, 1), by_lane)

    def harmonic(first, second):
        return 2.0 * first * second / (first + second)

    inside_low_g = jnp.where(g > 0, 1.0, 0.0)
    inside_high_g = jnp.where(g < NG - 1, 1.0, 0.0)
    inside_low_y = jnp.where(y > 0, 1.0, 0.0)
    inside_high_y = jnp.where(y < NY - 1, 1.0, 0.0)

    def faces(q):
        lo, n = LO - q, B + 2 * q

        whole = pl.ds(lo, n)
        fx[lo - 1, whole] = harmonic(kb[lo - 1, whole], kb[lo, whole])

        def fx_rows(step, _):
            i = lo + 2 * step
            low, high = harmonic(kb[i, whole], kb[i + 1, whole]), harmonic(kb[i + 1, whole], kb[i + 2, whole])
            fx[i, whole] = low
            fx[i + 1, whole] = high
            return 0
        lax.fori_loop(0, n // 2, fx_rows, 0)

        fx[LO - 1, pl.ds(lo, n)] = fx[LO - 1, pl.ds(lo, n)] * inside_low_g
        fx[HI - 1, pl.ds(lo, n)] = fx[HI - 1, pl.ds(lo, n)] * inside_high_g

        last = (iota(n, 1) == 7) & (iota(n, 2) == 127)

        def rows(step, _):
            first = lo + 2 * step
            done = []
            for i in (first, first + 1):
                own = kb[i, whole]
                low = harmonic(kb[i, lo - 1], kb[i, lo])
                along_j = harmonic(own, kb[i, pl.ds(lo + 1, n)])
                along_k = jnp.where(last, 0.0, harmonic(own, up(own)))
                done.append((low, along_j, along_k, cb[i, whole] + fx[i, whole] + fx[i - 1, whole] + along_k + down(along_k)))
            for i, (low, along_j, along_k, others) in enumerate(done):
                i = first + i
                fy[i, lo - 1] = low
                fy[i, whole] = along_j
                fz[i, whole] = along_k
                db[i, whole] = others
            return 0
        lax.fori_loop(0, n // 2, rows, 0)

        span = pl.ds(lo, n)
        fy[span, LO - 1] = fy[span, LO - 1] * inside_low_y
        fy[span, HI - 1] = fy[span, HI - 1] * inside_high_y

        def diagonal_row(i, _):
            db[i, whole] = db[i, whole] + fy[i, whole] + fy[i, pl.ds(lo - 1, n)]
            return 0
        lax.fori_loop(lo, lo + n, diagonal_row, 0)

    def applied(v, i, j0, c):
        at = pl.ds(j0, c)
        own, z = v[i, at], fz[i, at]
        return (
            db[i, at] * own
            - fx[i, at] * v[i + 1, at]
            - fx[i - 1, at] * v[i - 1, at]
            - fy[i, at] * v[i, pl.ds(j0 + 1, c)]
            - fy[i, pl.ds(j0 - 1, c)] * v[i, pl.ds(j0 - 1, c)]
            - z * up(own)
            - down(z * own)
        )

    def first_residual(x, dst):
        at = pl.ds(LO, B)
        done = [fb[i, at] + (cb[i, at] * x[i, at] - applied(x, i, LO, B)) for i in range(LO, HI)]
        for i, value in enumerate(done):
            dst[LO + i, at] = value

    for copy in x0_moves + k_moves[:4]:
        copy.wait_recv()
    for copy in k_relayed:
        copy.start()
    faces(0)

    def bound_row(i, carry):
        most, least = carry
        at = pl.ds(LO, B)
        c = cb[i, at]
        return (
            jnp.maximum(most, jnp.max(2.0 * db[i, at] - c, axis=0)),
            jnp.maximum(least, jnp.max(-c, axis=0)),
        )
    neg = jnp.full((8, 128), -3.0e38, F32)
    most, least = lax.fori_loop(LO, HI, bound_row, (neg, neg))
    sub = lax.broadcasted_iota(jnp.int32, (8, 128), 0)

    def over_rows(v):
        return jnp.broadcast_to(jnp.max(v, axis=0, keepdims=True), (8, 128))

    arst[0] = jnp.where(sub < 4, over_rows(most), over_rows(least))
    ar1[y] = arst[0]
    ar1_moves = [
        pltpu.make_async_remote_copy(
            src_ref=arst.at[0], dst_ref=ar1.at[y], send_sem=a1s.at[k], recv_sem=a1r.at[k],
            device_id=peer, device_id_type=MESH,
        )
        for k, peer in enumerate(along_y)
    ]
    for copy in ar1_moves:
        copy.start()

    first_residual(xb, v0)
    v0_moves, v0_relayed = halo(v0, 6, 3)
    for copy in v0_moves:
        copy.start()

    send_u((1, 3, 5, 15))
    relay_start(c_moves, c_relayed)
    for copy in ar1_moves:
        copy.wait_recv()
    arst[1] = jnp.max(ar1[...], axis=0)
    ar2[g] = arst[1]
    ar2_moves = [
        pltpu.make_async_remote_copy(
            src_ref=arst.at[1], dst_ref=ar2.at[g], send_sem=a2s.at[k], recv_sem=a2r.at[k],
            device_id=peer, device_id_type=MESH,
        )
        for k, peer in enumerate(along_g)
    ]
    for copy in ar2_moves:
        copy.start()
    for copy in c_moves[2:] + c_relayed + k_moves[4:] + k_relayed:
        copy.wait_recv()
    faces(5)

    for copy in ar2_moves:
        copy.wait_recv()
    send_u((7, 13, 2, 10))
    for copy in beta_planes:
        copy.wait()
    beta[0] = beta[0] * inside_low_g
    beta[B + 1] = beta[B + 1] * inside_high_g

    bounds = jnp.max(jnp.max(ar2[...], axis=0), axis=1, keepdims=True)
    high = jnp.broadcast_to(bounds[0:1], (8, 128))
    low = -jnp.broadcast_to(bounds[4:5], (8, 128))
    theta = (high + low) / 2.0
    delta = (high - low) / 2.0
    sigma = theta / delta
    rho = 1.0 / sigma
    coefs[0] = 1.0 / theta
    for turn in range(LEVELS):
        rho_new = 1.0 / (2.0 * sigma - rho)
        coefs[1 + 2 * turn] = rho_new * rho
        coefs[2 + 2 * turn] = 2.0 * rho_new / delta * theta
        rho = rho_new

    def level(src, turn, qi, qj):
        lo, n = LO - qi, B + 2 * qi
        rows = max(d for d in range(1, 19) if n % d == 0)
        j0, c = LO - qj, B + 2 * qj
        at = pl.ds(j0, c)
        inv, alpha, bet = coefs[0], coefs[1 + 2 * turn], coefs[2 + 2 * turn]
        before = src if turn == 0 else rb

        def some_rows(step, _):
            first = lo + step * rows
            done = []
            for i in range(rows):
                resid = before[first + i, at] - inv[None] * applied(src, first + i, j0, c)
                done.append((resid, alpha[None] * src[first + i, at] + bet[None] * resid))
            for i, (resid, value) in enumerate(done):
                rb[first + i, at] = resid
                e[turn, first + i, at] = value
            return 0
        lax.fori_loop(0, n // rows, some_rows, 0)

    def heat_step(start, qi, qj):
        src = start
        for turn in range(LEVELS):
            level(src, turn, qi - 1 - turn, qj - 1 - turn)
            src = e.at[turn]

    def summed(start, i, at):
        total = start[i, at]
        for turn in range(LEVELS):
            total = total + e[turn, i, at]
        return xb[i, at] + coefs[0][None] * total

    relay(v0_moves, v0_relayed, (9, 11))
    heat_step(v0, 6, 6)

    for copy in x0_moves:
        copy.wait_send()

    for i in range(LO - 1, HI + 1):
        at = pl.ds(LO - 1, B + 2)
        xb[i, at] = summed(v0, i, at)

    first_residual(xb, v1)
    v1_moves, v1_relayed = halo(v1, 6, 4, 5)
    for copy in v1_moves:
        copy.start()
    relay(v1_moves, v1_relayed, (6, 14))
    heat_step(v1, 6, 5)

    for i in range(B + 2):
        ytr[i] = summed(v1, LO - 1 + i, pl.ds(LO, B)).reshape(B * 8, 128)
    for i in range(B + 2):
        for kt in range(KT):
            natt[i, kt + 1] = ytr[i, pl.ds(kt, 8, stride=8), :]

    def t_copies(k):
        p = shifted(k)
        peer = (g, p)
        return [
            pltpu.make_async_remote_copy(
                src_ref=tst.at[p], dst_ref=t.at[:, rows_of_me],
                send_sem=ts.at[k], recv_sem=tr.at[k], device_id=peer, device_id_type=MESH,
            )
        ]

    t_moves = [t_copies(k) for k in range(1, NY)]
    t_own = [
        pltpu.make_async_copy(tst.at[y], t.at[:, rows_of_me], ts.at[0]),
    ]
    for group in ((10, 6, 9, 11), (14, 2, 5, 7), (13, 15, 8, 3), (1, 4, 12, 0)):
        done = []
        for k in group:
            p = shifted(k)
            cut = cuts(p)
            edge = zero_tile
            windows = []
            for i in range(B + 2):
                window, edge = pack(natt.at[i], cut, i, edge)
                windows.append(window)
            done.append((k, p, windows + [edge]))
        for k, p, windows in done:
            for i, window in enumerate(windows):
                tst[p, i] = window
            for copy in t_own if k == 0 else t_moves[k - 1]:
                copy.start()

    for kt in range(KT):
        t_out[:, :, pl.ds(kt * 128, 128)] = natt[pl.ds(1, B), kt + 1]

    for copy in u_own:
        copy.wait()
    for copies in u_moves:
        for copy in copies:
            copy.wait_recv()
    inner = pl.ds(8, 128)

    u_planes = plane_copies(u, lambda i: (slice(None), i, inner), ps, pr)
    for copy in u_planes:
        copy.start()

    length = tally[y]
    wide_lane = lax.broadcasted_iota(jnp.int32, (128, 128), 1)
    edges = ue[inner]

    def disp(a, i):
        own = u[a, i + 1, inner]
        plus, minus = beside(own, edges, a * 8 + i, length, wide_lane)
        total = (
            u[a, i + 2, inner] + u[a, i, inner] + u[a, i + 1, pl.ds(9, 128)] + u[a, i + 1, pl.ds(7, 128)]
            + plus + minus
        )
        return mu[i] * (6.0 * own - total)

    for a in range(3):
        def disp_rows(step, _, a=a):
            first = 1 + 2 * step
            done = [disp(a, first), disp(a, first + 1)]
            for i, value in enumerate(done):
                r_out[a, first + i] = value
            return 0
        lax.fori_loop(0, B // 2 - 1, disp_rows, 0)

    for copy in u_planes:
        copy.wait_recv()
    for a in range(3):
        u[a, 0, inner] = u[a, 0, inner] * inside_low_g
        u[a, B + 1, inner] = u[a, B + 1, inner] * inside_high_g
        done = [disp(a, 0), disp(a, B - 1)]
        r_out[a, 0] = done[0]
        r_out[a, B - 1] = done[1]

    valid = wide_lane < length

    for copy in t_own:
        copy.wait()
    for copies in t_moves:
        for copy in copies:
            copy.wait_recv()

    for i in range(B + 2):
        t[i, inner] = beta[i] * t[i, inner]

    def stress_rows(step, _):
        done = []
        for i in (2 * step, 2 * step + 1):
            plus, minus = beside(t[i + 1, inner], beta[i + 1] * t[B + 2, inner], i + 1, length, wide_lane)
            along_i = t[i + 2, inner] - t[i, inner]
            along_j = t[i + 1, pl.ds(9, 128)] - t[i + 1, pl.ds(7, 128)]
            for a, v in enumerate((along_i, along_j, plus - minus)):
                done.append((a, i, jnp.where(valid, r_out[a, i] + 0.5 * v, 0.0)))
        for a, i, value in done:
            r_out[a, i] = value
        return 0
    lax.fori_loop(0, B // 2, stress_rows, 0)

    for copy in k_moves + k_relayed + c_moves + c_relayed + v0_moves + v0_relayed + v1_moves + v1_relayed:
        copy.wait_send()
    for copy in ar1_moves + ar2_moves + u_planes:
        copy.wait_send()
    for copies in u_moves + t_moves:
        for copy in copies:
            copy.wait_send()


def beside(own, edges, at, length, lane):
    nxt = pltpu.roll(edges, (length - 1 - 32 - at + 256) & 127, 1)
    prev = pltpu.roll(edges, (128 - at) & 127, 1)
    plus = jnp.where(lane == length - 1, nxt, pltpu.roll(own, 127, 1))
    minus = jnp.where(lane == 0, prev, pltpu.roll(own, 1, 1))
    return plus, minus


def local(
    starting_warmth_level,
    diffusive_coefficient_map,
    specific_warmth_store,
    energy_source_flux,
    deformation_vector,
    substance_label_columns,
    substance_moduli_table,
    subdomain_point_tally,
):
    hbm = pl.BlockSpec(memory_space=pl.ANY)
    vmem = pl.BlockSpec(memory_space=pltpu.VMEM)
    smem = pl.BlockSpec(memory_space=pltpu.SMEM)
    grid = pltpu.VMEM((N, N, 8, 128), F32)
    dma = pltpu.SemaphoreType.DMA
    return pl.pallas_call(
        kernel,
        out_shape=(
            pltpu.VMEM((B, B, KT * 128), F32),
            pltpu.VMEM((3, B, NY * 8, ZMAX), F32),
        ),
        in_specs=[hbm] * 5 + [vmem, smem, smem],
        out_specs=(vmem, vmem),
        scratch_shapes=[
            pltpu.VMEM((4, B, KT * 8, 128), F32),
            pltpu.VMEM((3, B, KT + 2, 8, 128), F32),
            grid, grid, grid, grid, grid, grid,
            pltpu.VMEM((LEVELS, N, N, 8, 128), F32),
            grid, grid, grid, grid, grid,
            pltpu.VMEM((NY, 3, B, 8, 128), F32),
            pltpu.VMEM((NY, 8, 128), F32),
            pltpu.VMEM((3, B + 2, 8 + 128 + 8, 128), F32),
            pltpu.VMEM((8 + 128 + 8, 128), F32),
            pltpu.VMEM((NY, B + 3, 8, 128), F32),
            pltpu.VMEM((B + 3, 8 + 128 + 8, 128), F32),
            pltpu.VMEM((B + 2, KT + 2, 8, 128), F32),
            pltpu.VMEM((B + 2, B * 8, 128), F32),
            pltpu.VMEM((B, 128, 128), F32),
            pltpu.VMEM((B + 2, 128, 128), F32),
            pltpu.VMEM((NY, 8, 128), F32),
            pltpu.VMEM((NG, 8, 128), F32),
            pltpu.VMEM((2, 8, 128), F32),
            pltpu.VMEM((1 + 2 * LEVELS, 8, 128), F32),
            pltpu.SMEM((NY,), jnp.int32),
            dma((4, KT)), dma((KT,)),
            dma((5, 12)), dma((5, 12)),
            dma((NY - 1,)), dma((NY - 1,)), dma((NG - 1,)), dma((NG - 1,)),
            dma((NY,)), dma((NY,)), dma((NY,)), dma((NY,)),
            dma((NY,)), dma((NY,)),
            dma((2,)), dma((2,)), dma((2,)), dma((2,)),
        ],
        compiler_params=pltpu.CompilerParams(
            collective_id=0, has_side_effects=True, vmem_limit_bytes=60 * 2**20
        ),
    )(
        starting_warmth_level,
        diffusive_coefficient_map,
        specific_warmth_store,
        energy_source_flux,
        deformation_vector,
        substance_label_columns,
        substance_moduli_table,
        subdomain_point_tally,
    )


def solution(mesh):
    placed = (
        P("gx", "yz", None),
        P("gx", "yz", None),
        P("gx", "yz", None),
        P("gx", "yz", None),
        P(None, "gx", "yz", None),
        P("gx", None),
        P(),
        P(),
    )
    return jax.shard_map(
        local,
        mesh=mesh,
        in_specs=placed,
        out_specs=(P("gx", "yz", None), P(None, "gx", None, "yz")),
        check_vma=False,
    )
```
